32 devices in a mesh: own: 16 (over z, x, core), pair: 2 (over y).
Axes of the slice: x: 2, y: 2, z: 4, core: 2. Of those that a mesh axis runs over, the one named last changes fastest.
Arguments:
- embeddings: float32 [32, 128, 1024], P('own'), as said below
- cluster_sizes: int32 [8], replicated, may hold values from 1 to 12, 32 in all
- row_counts: int32 [32], replicated, may hold values from 32 to 128, as said below
Outputs:
- near_sums: bfloat16 [32, 128, 1024], P('own', 'pair')
- log_masses: float32 [32, 128], P('own', 'pair')
The draws below stay inside these ranges and needn't reach their ends.
Inputs may be any that keep to these rules, and one draw needn't show every extreme that they name: `row_counts`: some block has all 128 valid rows. `embeddings`: finite rows of nonzero norm.
All inputs are finite; a program needn't handle non-finite values.
Results may differ from the reference program's by a relative error of at most 0.01.
Values may be sent and summed in bfloat16 or wider, within the bound.
A program may use at most 64 MiB of HBM per device.

```python
import math
import jax
import jax.numpy as jnp
import numpy as np
from jax import lax

W = 1024
R = 128
SPAN = 12
BLOCKS = 32
CLUSTERS = 8


def draw_embeddings(key, part):
    subkeys = jax.random.split(key, 1)
    base_rows = jax.random.normal(subkeys[0], (BLOCKS, R, W), jnp.float32)
    return base_rows


def draw_row_counts(key, part):
    first_key, second_key = jax.random.split(key)
    counts = jax.random.randint(first_key, (BLOCKS,), max(2, R // 4), R + 1)
    full_block = jax.random.randint(second_key, (), 0, BLOCKS)
    return jnp.where(jnp.arange(BLOCKS) == full_block, R, counts).astype(jnp.int32)


def split_up(count, total, reach, lean):
    weights = [(1 << 20) // math.isqrt(standing ** lean) + 1 for standing in range(2, count + 1)]
    surplus, given = total - reach - (count - 1), [1] * (count - 1)
    while surplus > 0:
        candidates = [i for i in range(count - 1) if given[i] < reach]
        mass, remaining = sum([weights[i] for i in candidates]), surplus
        for i in candidates:
            extra = min(reach - given[i], max(1, remaining * weights[i] // mass), surplus)
            given[i] = given[i] + extra
            surplus = surplus - extra
    return np.array([reach] + given)


def ragged(rng, count, total, bound, slope):
    if count == 2:
        one = jax.random.randint(rng, (), max(1, total - bound), min(bound, total - 1) + 1)
        return jnp.stack([one, total - one])
    lengths = jnp.asarray(split_up(count, total, bound, slope), jnp.int32)
    couples = (count - 1) // 2
    donor, receiver = lengths[1:1 + 2 * couples:2], lengths[2:2 + 2 * couples:2]
    margin = jnp.minimum(donor - 1, bound - receiver)
    passed = jax.random.randint(jax.random.fold_in(rng, 1), (couples,), 0, 1 << 20) % (margin + 1)
    lengths = lengths.at[1:1 + 2 * couples:2].set(donor - passed).at[2:2 + 2 * couples:2].set(receiver + passed)
    return lengths[jax.random.permutation(jax.random.fold_in(rng, 2), count)]


def setup_inputs(seed: int = 0) -> dict:
    key_of = jax.random.split(jax.random.key(seed), 4)
    return {
        "embeddings": draw_embeddings(jax.random.fold_in(key_of[3], 71), 0),
        "cluster_sizes": ragged(key_of[1], CLUSTERS, BLOCKS, SPAN, 2).astype(jnp.int32),
        "row_counts": draw_row_counts(jax.random.fold_in(key_of[3], 71), 0),
    }


sharpness = 128.0
negative = -1e+30

def unit_rows(values):
    squares = lax.optimization_barrier(jnp.sum(values * values, axis=-1, keepdims=True))
    return (values * lax.rsqrt(squares + 1e-06)).astype(jnp.bfloat16)

def reference(embeddings, cluster_sizes, row_counts):
    normed = unit_rows(embeddings)
    cluster_start = jnp.cumsum(cluster_sizes) - cluster_sizes
    block_ids = jnp.arange(BLOCKS, dtype=jnp.int32)
    owner_cluster = lax.optimization_barrier(jnp.sum((block_ids[:, None] >= cluster_start[None, :]).astype(jnp.int32), axis=1)) - 1
    row_index = jnp.arange(R, dtype=jnp.int32)

    def one_block(block):
        queries = normed[block]

        def tile_step(carried, offset):
            source = block + offset
            inside = (source >= 0) & (source < BLOCKS)
            clipped = jnp.clip(source, 0, BLOCKS - 1).astype(jnp.int32)
            same_cluster = inside & (owner_cluster[clipped] == owner_cluster[block])

            def score_tile(running):
                run_max, run_mass, run_sum = running
                key_rows = normed[clipped]
                scores = sharpness * jnp.dot(queries, key_rows.T, preferred_element_type=jnp.float32)
                kept = (row_index[None, :] < row_counts[clipped]) & ((offset != 0) | (row_index[:, None] != row_index[None, :]))
                scores = jnp.where(kept, scores, negative)
                row_top = lax.optimization_barrier(jnp.max(scores, axis=1))
                weight = jnp.where(kept, jnp.exp(scores - row_top[:, None]), 0.0)
                partial_value = jnp.dot(weight.astype(jnp.bfloat16), key_rows, preferred_element_type=jnp.float32)
                new_max = jnp.maximum(run_max, row_top)
                old_scale = jnp.exp(run_max - new_max)
                new_scale = jnp.exp(row_top - new_max)
                return (new_max, run_mass * old_scale + lax.optimization_barrier(jnp.sum(weight, axis=1)) * new_scale, run_sum * old_scale[:, None] + partial_value * new_scale[:, None])
            return (lax.cond(same_cluster, score_tile, lambda running: running, carried), None)
        start_state = (jnp.full((R,), negative, jnp.float32), jnp.zeros((R,), jnp.float32), jnp.zeros((R, W), jnp.float32))
        offsets = jnp.arange(-(SPAN - 1), SPAN, dtype=jnp.int32)
        run_max, run_mass, run_sum = lax.scan(tile_step, start_state, offsets)[0]
        row_valid = row_index < row_counts[block]
        sums_here = jnp.where(row_valid[:, None], run_sum / run_mass[:, None], 0.0).astype(jnp.bfloat16)
        mass_here = jnp.where(row_valid, run_max + jnp.log(run_mass), 0.0)
        return (sums_here, mass_here)
    near_sums, log_masses = lax.map(one_block, block_ids)
    return (near_sums, log_masses)
```

```python
import functools

import jax
import jax.numpy as jnp
from jax import lax
from jax.experimental import pallas as pl
from jax.experimental.pallas import tpu as pltpu
from jax.sharding import PartitionSpec as P

SPAN = 12


sharpness = 128.0
negative = -1e30


def passed_along(shard, axis, by):
    count = lax.axis_size(axis)
    pairs = [(i, i + by) for i in range(count) if 0 <= i + by < count]
    return lax.ppermute(shard, axis, pairs)


def unit_rows(values):
    squares = jnp.sum(values * values, axis=-1, keepdims=True)
    return (values * lax.rsqrt(squares + 1e-06)).astype(jnp.bfloat16)


def fold_in(running, row_top, row_total, partial_value):
    run_max, run_mass, run_sum = running
    new_max = jnp.maximum(run_max, row_top)
    old_scale = jnp.exp(run_max - new_max)
    new_scale = jnp.exp(row_top - new_max)
    return (
        new_max,
        run_mass * old_scale + row_total * new_scale,
        run_sum * old_scale[..., None] + partial_value * new_scale[..., None],
    )


def combine_states(first_state, second_state):
    return fold_in(first_state, second_state[0], second_state[1], second_state[2])


def row_stats(scores, kept, key_rows):
    scores = jnp.where(kept, scores, negative)
    row_top = jnp.max(scores, axis=1)
    weight = jnp.where(kept, jnp.exp(scores - row_top[:, None]), 0.0)
    partial_value = jnp.dot(
        weight.astype(jnp.bfloat16), key_rows, preferred_element_type=jnp.float32
    )
    return (row_top, jnp.sum(weight, axis=1), partial_value)


def pick_entry(table, position):
    places = jnp.arange(table.shape[0], dtype=jnp.int32)
    return jnp.sum(jnp.where(places == position, table, 0))


def empty_state(row_total, feature_count):
    return (
        jnp.full((row_total,), negative, jnp.float32),
        jnp.zeros((row_total,), jnp.float32),
        jnp.zeros((row_total, feature_count), jnp.float32),
    )


def stack_states(states):
    return tuple((jnp.stack([state[field] for state in states]) for field in range(3)))


def own_rows(stacked, slice_rows, pair_count):
    run_max, run_mass, run_sum = stacked
    local_blocks = run_max.shape[0]
    feature_count = run_sum.shape[2]
    arrived = (
        lax.all_to_all(
            run_max.reshape(local_blocks, pair_count, slice_rows),
            "pair",
            split_axis=1,
            concat_axis=1,
            tiled=True,
        ),
        lax.all_to_all(
            run_mass.reshape(local_blocks, pair_count, slice_rows),
            "pair",
            split_axis=1,
            concat_axis=1,
            tiled=True,
        ),
        lax.all_to_all(
            run_sum.reshape(local_blocks, pair_count, slice_rows, feature_count),
            "pair",
            split_axis=1,
            concat_axis=1,
            tiled=True,
        ),
    )
    new_max = jnp.max(arrived[0], axis=1)
    scales = jnp.exp(arrived[0] - new_max[:, None, :])
    return (
        new_max,
        jnp.sum(arrived[1] * scales, axis=1),
        jnp.sum(arrived[2] * scales[..., None], axis=1),
    )


def body(embeddings, cluster_sizes, row_counts):
    normed = unit_rows(embeddings)
    local_blocks, block_rows, feature_count = normed.shape
    pair_count = lax.axis_size("pair")
    own_count = lax.axis_size("own")
    block_total = own_count * local_blocks
    slice_rows = block_rows // pair_count
    own_index = lax.axis_index("own")
    slice_start = lax.axis_index("pair") * slice_rows
    my_slice = lax.dynamic_slice_in_dim(normed, slice_start, slice_rows, 1)
    cluster_start = jnp.cumsum(cluster_sizes) - cluster_sizes
    block_ids = jnp.arange(block_total, dtype=jnp.int32)
    owner_cluster = (
        jnp.sum((block_ids[:, None] >= cluster_start[None, :]).astype(jnp.int32), axis=1) - 1
    )
    full_rows = jnp.arange(block_rows, dtype=jnp.int32)
    my_rows = slice_start + jnp.arange(slice_rows, dtype=jnp.int32)
    offset_count = (SPAN + local_blocks - 2) // local_blocks

    def block_of(owner, local):
        return owner * local_blocks + local

    def linked_to(query_block, source):
        inside = (source >= 0) & (source < block_total)
        return inside & (
            pick_entry(owner_cluster, source) == pick_entry(owner_cluster, query_block)
        )

    def key_mask(query_block, source):
        valid_keys = my_rows[None, :] < pick_entry(row_counts, source)
        not_self = (query_block != source) | (full_rows[:, None] != my_rows[None, :])
        return linked_to(query_block, source) & valid_keys & not_self

    def tile_scores(queries, key_rows):
        return sharpness * jnp.dot(queries, key_rows.T, preferred_element_type=jnp.float32)

    running = [empty_state(block_rows, feature_count) for local in range(local_blocks)]
    for local in range(local_blocks):
        query_block = block_of(own_index, local)
        for other in range(local_blocks):
            source = block_of(own_index, other)
            row_top, row_total, partial_value = row_stats(
                tile_scores(normed[local], my_slice[other]),
                key_mask(query_block, source),
                my_slice[other],
            )
            running[local] = fold_in(running[local], row_top, row_total, partial_value)
    column_state = [empty_state(slice_rows, feature_count) for local in range(local_blocks)]
    for offset in range(1, offset_count + 1):
        earlier = passed_along(my_slice, "own", offset)
        back_states = [empty_state(slice_rows, feature_count) for local in range(local_blocks)]
        for local in range(local_blocks):
            query_block = block_of(own_index, local)
            query_valid = full_rows < pick_entry(row_counts, query_block)
            for other in range(local_blocks):
                source = block_of(own_index - offset, other)
                scores = tile_scores(normed[local], earlier[other])
                row_top, row_total, partial_value = row_stats(
                    scores, key_mask(query_block, source), earlier[other]
                )
                running[local] = fold_in(running[local], row_top, row_total, partial_value)
                back_mask = (
                    linked_to(query_block, source) & query_valid[None, :] & (my_rows[:, None] >= 0)
                )
                back_top, back_total, back_sum = row_stats(scores.T, back_mask, normed[local])
                back_states[other] = fold_in(back_states[other], back_top, back_total, back_sum)
        stacked_back = stack_states(back_states)
        returned = passed_along((stacked_back[0], stacked_back[1], stacked_back[2]), "own", -offset)
        later_inside = own_index + offset < own_count
        for local in range(local_blocks):
            column_state[local] = fold_in(
                column_state[local],
                jnp.where(later_inside, returned[0][local], negative),
                jnp.where(later_inside, returned[1][local], 0.0),
                jnp.where(later_inside, returned[2][local], 0.0),
            )
    reduced = own_rows(stack_states(running), slice_rows, pair_count)
    result_state = combine_states(reduced, stack_states(column_state))
    run_max, run_mass, run_sum = result_state
    my_counts = jnp.stack(
        [pick_entry(row_counts, block_of(own_index, local)) for local in range(local_blocks)]
    )
    row_valid = my_rows[None, :] < my_counts[:, None]
    near_sums = jnp.where(row_valid[..., None], run_sum / run_mass[..., None], 0.0).astype(
        jnp.bfloat16
    )
    log_masses = jnp.where(row_valid, run_max + jnp.log(run_mass), 0.0)
    return (near_sums, log_masses)


MESH = pl.DeviceIdType.MESH


def kernel(
    groups, blocks, rows, slice_rows,
    sizes_ref, counts_ref, emb_ref, near_ref, mass_ref,
    queries, keys, top, mass, total,
    chip_out, chip_in, chip_stats_out, chip_stats_in,
    pair_out, pair_in, pair_stats_out, pair_stats_in,
    share_send, share_recv, direct_send, key_recv, relay_send,
    chip_send, chip_recv, chip_stats_send, chip_stats_recv,
    pair_send, pair_recv, pair_stats_send, pair_stats_recv,
):
    width = emb_ref.shape[2]
    mine = lax.axis_index("own")
    half = lax.axis_index("pair")
    group, core = mine // 2, mine % 2
    lane_x = group % 2
    toward = 1 - 2 * lane_x
    sibling = mine + 1 - 2 * core
    across = group + toward
    ahead, behind = group + 2 * toward, group - 2 * toward
    has_ahead = (ahead >= 0) & (ahead < groups)
    has_behind = (behind >= 0) & (behind < groups)
    behind2 = group - 4 * toward
    has_behind2 = (behind2 >= 0) & (behind2 < groups)
    zero_slot = 3
    slots = 2 * blocks
    half_rows = rows // 2
    query_rows = slots * rows

    def device(group_index, core_index):
        return (group_index * 2 + core_index, half)

    partner = (mine, 1 - half)

    barrier = pltpu.get_barrier_semaphore()

    def greet(target):
        pl.semaphore_signal(barrier, inc=1, device_id=target, device_id_type=MESH)

    greet(device(group, 1 - core))
    greet(partner)
    for other_core in range(2):
        greet(device(across, other_core))

    @pl.when(has_ahead)
    def _():
        for other_core in range(2):
            greet(device(ahead, other_core))

    @pl.when(has_behind)
    def _():
        for other_core in range(2):
            greet(device(behind, other_core))

    for local in range(blocks):
        values = emb_ref[local]
        squares = jnp.sum(values * values, axis=-1, keepdims=True)
        queries[core * blocks + local] = (values * lax.rsqrt(squares + 1e-06)).astype(jnp.bfloat16)

    own_blocks = pl.ds(core * blocks, blocks)

    def key_rows(core_index):
        return pl.ds(pl.multiple_of((half * 2 + core_index) * slice_rows, slice_rows), slice_rows)

    share = pltpu.make_async_remote_copy(
        src_ref=queries.at[own_blocks],
        dst_ref=queries.at[own_blocks],
        send_sem=share_send.at[0],
        recv_sem=share_recv.at[0],
        device_id=device(group, 1 - core),
        device_id_type=MESH,
    )
    share_in = pltpu.make_async_remote_copy(
        src_ref=queries.at[pl.ds((1 - core) * blocks, blocks)],
        dst_ref=queries.at[pl.ds((1 - core) * blocks, blocks)],
        send_sem=share_send.at[0],
        recv_sem=share_recv.at[0],
        device_id=device(group, 1 - core),
        device_id_type=MESH,
    )

    def direct(place, target, slot, other_core):
        return pltpu.make_async_remote_copy(
            src_ref=queries.at[own_blocks, key_rows(other_core)],
            dst_ref=keys.at[slot, core],
            send_sem=direct_send.at[place, other_core],
            recv_sem=key_recv.at[slot, core],
            device_id=device(target, other_core),
            device_id_type=MESH,
        )

    def relay(place, source_offset, target, target_offset, part):
        return pltpu.make_async_remote_copy(
            src_ref=keys.at[zero_slot + source_offset, part],
            dst_ref=keys.at[zero_slot + target_offset, part],
            send_sem=relay_send.at[place, part],
            recv_sem=key_recv.at[zero_slot + target_offset, part],
            device_id=device(target, core),
            device_id_type=MESH,
        )

    def arrived(offset, part):
        slot = zero_slot + offset
        pltpu.make_async_remote_copy(
            src_ref=keys.at[slot, part],
            dst_ref=keys.at[slot, part],
            send_sem=relay_send.at[0, part],
            recv_sem=key_recv.at[slot, part],
            device_id=device(across, core),
            device_id_type=MESH,
        ).wait_recv()

    def direct_across(other_core):
        return direct(0, across, zero_slot - toward, other_core)

    def direct_ahead(other_core):
        return direct(1, ahead, zero_slot - 2 * toward, other_core)

    def direct_behind(other_core):
        return direct(2, behind, zero_slot + 2 * toward, other_core)

    def relay_across(part):
        return relay(0, 2 * toward, across, toward, part)

    def relay_behind(part):
        return relay(1, toward, behind, 3 * toward, part)

    def relay_ahead(part):
        return relay(2, -toward, ahead, -3 * toward, part)

    neighbours = 4 + 2 * has_ahead.astype(jnp.int32) + 2 * has_behind.astype(jnp.int32)
    pl.semaphore_wait(barrier, neighbours)

    for other_core in range(2):
        direct_across(other_core).start()

        @pl.when(has_ahead)
        def _():
            direct_ahead(other_core).start()

        @pl.when(has_behind)
        def _():
            direct_behind(other_core).start()

    share.start()

    starts = []
    so_far = jnp.int32(0)
    for cluster in range(sizes_ref.shape[0]):
        starts.append(so_far)
        so_far = so_far + sizes_ref[cluster]

    def cluster_of(ids):
        return sum((ids >= start).astype(jnp.int32) for start in starts)

    row_ids = lax.broadcasted_iota(jnp.int32, (query_rows, 1), 0)
    query_cluster = cluster_of(group * slots + row_ids // rows)
    lane_ids = lax.broadcasted_iota(jnp.int32, (1, slots * slice_rows), 1)
    lane_block = lane_ids // slice_rows
    lane_row = lane_ids % slice_rows + (half * 2 + core) * slice_rows

    top[...] = jnp.full_like(top, negative)
    mass[...] = jnp.zeros_like(mass)
    total[...] = jnp.zeros_like(total)
    share_in.wait_recv()
    keys[zero_slot] = queries[:, key_rows(core), :].reshape(keys.shape[1:])

    def step(turn, carry):
        far = jnp.where(turn == 2, 2, jnp.where(turn == 3, -2, 0))
        near = jnp.where(turn == 1, 1, jnp.where(turn == 4, -1, 0))
        last = jnp.where(turn == 5, 3, jnp.where(turn == 6, -3, 0))
        offset = toward * (far + near + last)

        @pl.when(turn == 1)
        def _():
            for part in range(2):
                arrived(toward, part)

                @pl.when(has_behind)
                def _():
                    relay_behind(part).start()

            @pl.when(has_ahead)
            def _():
                for part in range(2):
                    arrived(2 * toward, part)
                    relay_across(part).start()

        @pl.when((turn == 3) & has_behind)
        def _():
            for part in range(2):
                arrived(-2 * toward, part)

        @pl.when((turn == 4) & has_behind)
        def _():
            for part in range(2):
                arrived(-toward, part)

                @pl.when(has_ahead)
                def _():
                    relay_ahead(part).start()

        @pl.when((turn == 5) & has_ahead)
        def _():
            for part in range(2):
                arrived(3 * toward, part)

        @pl.when((turn == 6) & has_behind2)
        def _():
            for part in range(2):
                arrived(-3 * toward, part)

        present = (group + offset >= 0) & (group + offset < groups)

        @pl.when(present)
        def _():
            first_block = (group + offset) * slots
            valid = jnp.zeros_like(lane_ids)
            for local in range(slots):
                valid = jnp.where(lane_block == local, counts_ref[first_block + local], valid)
            key_cluster = jnp.where(lane_row < valid, cluster_of(first_block + lane_block), -1)
            self_row = jnp.where(offset == 0, lane_block * rows + lane_row, -1)
            block_keys = keys[zero_slot + offset].reshape(slots * slice_rows, width)
            scores = sharpness * lax.dot_general(
                queries[...].reshape(query_rows, width), block_keys,
                (((1,), (1,)), ((), ())), preferred_element_type=jnp.float32,
            )
            kept = (query_cluster == key_cluster) & (row_ids != self_row)
            scores = jnp.where(kept, scores, 2.0 * negative)
            new_top = jnp.maximum(top[...], jnp.max(scores, axis=1, keepdims=True))
            scale = jnp.exp(top[...] - new_top)
            weight = jnp.exp(scores - new_top)
            top[...] = new_top
            mass[...] = mass[...] * scale + jnp.sum(weight, axis=1, keepdims=True)
            weight = weight.astype(jnp.bfloat16)
            piece = min(256, width)
            for column in range(0, width, piece):
                total[:, column:column + piece] = total[:, column:column + piece] * scale + jnp.dot(
                    weight, block_keys[:, column:column + piece], preferred_element_type=jnp.float32
                )

        return carry

    lax.fori_loop(0, 7, step, 0)

    eye = (
        lax.broadcasted_iota(jnp.int32, (half_rows, half_rows), 0)
        == lax.broadcasted_iota(jnp.int32, (half_rows, half_rows), 1)
    )

    def to_lanes(column):
        return jnp.sum(jnp.where(eye, column, 0.0), axis=0, keepdims=True)

    def to_rows(lanes):
        return jnp.sum(jnp.where(eye, lanes, 0.0), axis=1, keepdims=True)

    def rows_of(block, side):
        return pl.ds(pl.multiple_of(block * rows + side * half_rows, half_rows), half_rows)

    def chip_copy(piece):
        return (
            pltpu.make_async_remote_copy(
                src_ref=chip_stats_out.at[piece], dst_ref=chip_stats_in.at[piece],
                send_sem=chip_stats_send.at[piece], recv_sem=chip_stats_recv.at[piece],
                device_id=device(group, 1 - core), device_id_type=MESH,
            ),
            pltpu.make_async_remote_copy(
                src_ref=chip_out.at[piece], dst_ref=chip_in.at[piece],
                send_sem=chip_send.at[piece], recv_sem=chip_recv.at[piece],
                device_id=device(group, 1 - core), device_id_type=MESH,
            ),
        )

    def pair_copy(local):
        return (
            pltpu.make_async_remote_copy(
                src_ref=pair_stats_out.at[local], dst_ref=pair_stats_in.at[local],
                send_sem=pair_stats_send.at[local], recv_sem=pair_stats_recv.at[local],
                device_id=partner, device_id_type=MESH,
            ),
            pltpu.make_async_remote_copy(
                src_ref=pair_out.at[local], dst_ref=pair_in.at[local],
                send_sem=pair_send.at[local], recv_sem=pair_recv.at[local],
                device_id=partner, device_id_type=MESH,
            ),
        )

    pieces = [(remote, local) for remote in range(2) for local in range(blocks)]

    def side_of(remote):
        return 1 - half if remote == 0 else half

    for index, (remote, local) in enumerate(pieces):
        span = rows_of((1 - core) * blocks + local, side_of(remote))
        chip_out[index] = total[span].astype(jnp.bfloat16)
        chip_stats_out[index, 0:1, :half_rows] = to_lanes(top[span])
        chip_stats_out[index, 1:2, :half_rows] = to_lanes(mass[span])
        for copy in chip_copy(index):
            copy.start()

    for index, (remote, local) in enumerate(pieces):
        for copy in chip_copy(index):
            copy.wait_recv()
        span = rows_of(core * blocks + local, side_of(remote))
        other_top = to_rows(chip_stats_in[index, 0:1, :half_rows])
        other_mass = to_rows(chip_stats_in[index, 1:2, :half_rows])
        new_top = jnp.maximum(top[span], other_top)
        scale = jnp.exp(top[span] - new_top)
        other_scale = jnp.exp(other_top - new_top)
        new_mass = mass[span] * scale + other_mass * other_scale
        new_total = total[span] * scale + chip_in[index].astype(jnp.float32) * other_scale
        if remote == 0:
            pair_out[local] = new_total.astype(jnp.bfloat16)
            pair_stats_out[local, 0:1, :half_rows] = to_lanes(new_top)
            pair_stats_out[local, 1:2, :half_rows] = to_lanes(new_mass)
            for copy in pair_copy(local):
                copy.start()
        else:
            total[span] = new_total
            top[span] = new_top
            mass[span] = new_mass

    place = lax.broadcasted_iota(jnp.int32, (half_rows, 1), 0) + half * half_rows
    for local in range(blocks):
        for copy in pair_copy(local):
            copy.wait_recv()
        span = rows_of(core * blocks + local, half)
        other_top = to_rows(pair_stats_in[local, 0:1, :half_rows])
        other_mass = to_rows(pair_stats_in[local, 1:2, :half_rows])
        new_top = jnp.maximum(top[span], other_top)
        scale = jnp.exp(top[span] - new_top)
        other_scale = jnp.exp(other_top - new_top)
        new_mass = mass[span] * scale + other_mass * other_scale
        row_valid = place < counts_ref[mine * blocks + local]
        own_part = total[span] * (scale / new_mass)
        other_part = pair_in[local].astype(jnp.float32) * (other_scale / new_mass)
        near_ref[local] = jnp.where(row_valid, own_part + other_part, 0.0).astype(jnp.bfloat16)
        logs = jnp.where(row_valid, new_top + jnp.log(new_mass), 0.0)
        mass_ref[local:local + 1, :] = to_lanes(logs)

    share.wait_send()
    for other_core in range(2):
        direct_across(other_core).wait_send()

        @pl.when(has_ahead)
        def _():
            direct_ahead(other_core).wait_send()
            relay_across(other_core).wait_send()

        @pl.when(has_behind)
        def _():
            direct_behind(other_core).wait_send()
            relay_behind(other_core).wait_send()

        @pl.when(has_ahead & has_behind)
        def _():
            relay_ahead(other_core).wait_send()

    for index in range(len(pieces)):
        for copy in chip_copy(index):
            copy.wait_send()
    for local in range(blocks):
        for copy in pair_copy(local):
            copy.wait_send()


def kernel_body(embeddings, cluster_sizes, row_counts):
    blocks, rows, width = embeddings.shape
    groups = lax.axis_size("own") // 2
    slots, slice_rows, half_rows = 2 * blocks, rows // 4, rows // 2
    query_rows = slots * rows
    wide, narrow = jnp.float32, jnp.bfloat16
    stats = (8, 128)
    dma = pltpu.SemaphoreType.DMA
    smem, vmem = pl.BlockSpec(memory_space=pltpu.SMEM), pl.BlockSpec(memory_space=pltpu.VMEM)
    return pl.pallas_call(
        functools.partial(kernel, groups, blocks, rows, slice_rows),
        out_shape=(
            jax.ShapeDtypeStruct((blocks, half_rows, width), narrow),
            jax.ShapeDtypeStruct((blocks, half_rows), wide),
        ),
        in_specs=[smem, smem, vmem],
        out_specs=(vmem, vmem),
        scratch_shapes=[
            pltpu.VMEM((slots, rows, width), narrow),
            pltpu.VMEM((7, 2, blocks, slice_rows, width), narrow),
            pltpu.VMEM((query_rows, 1), wide),
            pltpu.VMEM((query_rows, 1), wide),
            pltpu.VMEM((query_rows, width), wide),
            pltpu.VMEM((2 * blocks, half_rows, width), narrow),
            pltpu.VMEM((2 * blocks, half_rows, width), narrow),
            pltpu.VMEM((2 * blocks, *stats), wide),
            pltpu.VMEM((2 * blocks, *stats), wide),
            pltpu.VMEM((blocks, half_rows, width), narrow),
            pltpu.VMEM((blocks, half_rows, width), narrow),
            pltpu.VMEM((blocks, *stats), wide),
            pltpu.VMEM((blocks, *stats), wide),
            dma((1,)), dma((1,)),
            dma((3, 2)), dma((7, 2)), dma((3, 2)),
            dma((2 * blocks,)), dma((2 * blocks,)), dma((2 * blocks,)), dma((2 * blocks,)),
            dma((blocks,)), dma((blocks,)), dma((blocks,)), dma((blocks,)),
        ],
        compiler_params=pltpu.CompilerParams(
            collective_id=0, has_side_effects=True, vmem_limit_bytes=40 * 1024 * 1024
        ),
        cost_estimate=pl.CostEstimate(
            flops=4 * query_rows * 7 * slots * slice_rows * width,
            bytes_accessed=embeddings.size * 4,
            transcendentals=query_rows * 7 * slots * slice_rows,
        ),
    )(cluster_sizes, row_counts, embeddings)


def fits_kernel(block_shape):
    blocks, rows, width = block_shape
    covered = (SPAN + 2 * blocks - 2) // (2 * blocks) <= 3
    whole_tiles = rows % 128 == 0 and width % 128 == 0
    return lax.axis_size("pair") == 2 and lax.axis_size("own") % 4 == 0 and covered and whole_tiles


def device_part(embeddings, cluster_sizes, row_counts):
    chosen = kernel_body if fits_kernel(embeddings.shape) else body
    return chosen(embeddings, cluster_sizes, row_counts)


def solution(mesh):
    placed = (P("own", None, None), P(), P())
    return jax.shard_map(
        device_part,
        mesh=mesh,
        in_specs=placed,
        out_specs=(P("own", "pair", None), P("own", "pair")),
        check_vma=False,
    )
```

```python
import functools

import jax
import jax.numpy as jnp
from jax import lax
from jax.experimental import pallas as pl
from jax.experimental.pallas import tpu as pltpu
from jax.sharding import PartitionSpec as P

SPAN = 12


sharpness = 128.0
negative = -1e30


def passed_along(shard, axis, by):
    count = lax.axis_size(axis)
    pairs = [(i, i + by) for i in range(count) if 0 <= i + by < count]
    return lax.ppermute(shard, axis, pairs)


def unit_rows(values):
    squares = jnp.sum(values * values, axis=-1, keepdims=True)
    return (values * lax.rsqrt(squares + 1e-06)).astype(jnp.bfloat16)


def fold_in(running, row_top, row_total, partial_value):
    run_max, run_mass, run_sum = running
    new_max = jnp.maximum(run_max, row_top)
    old_scale = jnp.exp(run_max - new_max)
    new_scale = jnp.exp(row_top - new_max)
    return (
        new_max,
        run_mass * old_scale + row_total * new_scale,
        run_sum * old_scale[..., None] + partial_value * new_scale[..., None],
    )


def combine_states(first_state, second_state):
    return fold_in(first_state, second_state[0], second_state[1], second_state[2])


def row_stats(scores, kept, key_rows):
    scores = jnp.where(kept, scores, negative)
    row_top = jnp.max(scores, axis=1)
    weight = jnp.where(kept, jnp.exp(scores - row_top[:, None]), 0.0)
    partial_value = jnp.dot(
        weight.astype(jnp.bfloat16), key_rows, preferred_element_type=jnp.float32
    )
    return (row_top, jnp.sum(weight, axis=1), partial_value)


def pick_entry(table, position):
    places = jnp.arange(table.shape[0], dtype=jnp.int32)
    return jnp.sum(jnp.where(places == position, table, 0))


def empty_state(row_total, feature_count):
    return (
        jnp.full((row_total,), negative, jnp.float32),
        jnp.zeros((row_total,), jnp.float32),
        jnp.zeros((row_total, feature_count), jnp.float32),
    )


def stack_states(states):
    return tuple((jnp.stack([state[field] for state in states]) for field in range(3)))


def own_rows(stacked, slice_rows, pair_count):
    run_max, run_mass, run_sum = stacked
    local_blocks = run_max.shape[0]
    feature_count = run_sum.shape[2]
    arrived = (
        lax.all_to_all(
            run_max.reshape(local_blocks, pair_count, slice_rows),
            "pair",
            split_axis=1,
            concat_axis=1,
            tiled=True,
        ),
        lax.all_to_all(
            run_mass.reshape(local_blocks, pair_count, slice_rows),
            "pair",
            split_axis=1,
            concat_axis=1,
            tiled=True,
        ),
        lax.all_to_all(
            run_sum.reshape(local_blocks, pair_count, slice_rows, feature_count),
            "pair",
            split_axis=1,
            concat_axis=1,
            tiled=True,
        ),
    )
    new_max = jnp.max(arrived[0], axis=1)
    scales = jnp.exp(arrived[0] - new_max[:, None, :])
    return (
        new_max,
        jnp.sum(arrived[1] * scales, axis=1),
        jnp.sum(arrived[2] * scales[..., None], axis=1),
    )


def body(embeddings, cluster_sizes, row_counts):
    normed = unit_rows(embeddings)
    local_blocks, block_rows, feature_count = normed.shape
    pair_count = lax.axis_size("pair")
    own_count = lax.axis_size("own")
    block_total = own_count * local_blocks
    slice_rows = block_rows // pair_count
    own_index = lax.axis_index("own")
    slice_start = lax.axis_index("pair") * slice_rows
    my_slice = lax.dynamic_slice_in_dim(normed, slice_start, slice_rows, 1)
    cluster_start = jnp.cumsum(cluster_sizes) - cluster_sizes
    block_ids = jnp.arange(block_total, dtype=jnp.int32)
    owner_cluster = (
        jnp.sum((block_ids[:, None] >= cluster_start[None, :]).astype(jnp.int32), axis=1) - 1
    )
    full_rows = jnp.arange(block_rows, dtype=jnp.int32)
    my_rows = slice_start + jnp.arange(slice_rows, dtype=jnp.int32)
    offset_count = (SPAN + local_blocks - 2) // local_blocks

    def block_of(owner, local):
        return owner * local_blocks + local

    def linked_to(query_block, source):
        inside = (source >= 0) & (source < block_total)
        return inside & (
            pick_entry(owner_cluster, source) == pick_entry(owner_cluster, query_block)
        )

    def key_mask(query_block, source):
        valid_keys = my_rows[None, :] < pick_entry(row_counts, source)
        not_self = (query_block != source) | (full_rows[:, None] != my_rows[None, :])
        return linked_to(query_block, source) & valid_keys & not_self

    def tile_scores(queries, key_rows):
        return sharpness * jnp.dot(queries, key_rows.T, preferred_element_type=jnp.float32)

    running = [empty_state(block_rows, feature_count) for local in range(local_blocks)]
    for local in range(local_blocks):
        query_block = block_of(own_index, local)
        for other in range(local_blocks):
            source = block_of(own_index, other)
            row_top, row_total, partial_value = row_stats(
                tile_scores(normed[local], my_slice[other]),
                key_mask(query_block, source),
                my_slice[other],
            )
            running[local] = fold_in(running[local], row_top, row_total, partial_value)
    column_state = [empty_state(slice_rows, feature_count) for local in range(local_blocks)]
    for offset in range(1, offset_count + 1):
        earlier = passed_along(my_slice, "own", offset)
        back_states = [empty_state(slice_rows, feature_count) for local in range(local_blocks)]
        for local in range(local_blocks):
            query_block = block_of(own_index, local)
            query_valid = full_rows < pick_entry(row_counts, query_block)
            for other in range(local_blocks):
                source = block_of(own_index - offset, other)
                scores = tile_scores(normed[local], earlier[other])
                row_top, row_total, partial_value = row_stats(
                    scores, key_mask(query_block, source), earlier[other]
                )
                running[local] = fold_in(running[local], row_top, row_total, partial_value)
                back_mask = (
                    linked_to(query_block, source) & query_valid[None, :] & (my_rows[:, None] >= 0)
                )
                back_top, back_total, back_sum = row_stats(scores.T, back_mask, normed[local])
                back_states[other] = fold_in(back_states[other], back_top, back_total, back_sum)
        stacked_back = stack_states(back_states)
        returned = passed_along((stacked_back[0], stacked_back[1], stacked_back[2]), "own", -offset)
        later_inside = own_index + offset < own_count
        for local in range(local_blocks):
            column_state[local] = fold_in(
                column_state[local],
                jnp.where(later_inside, returned[0][local], negative),
                jnp.where(later_inside, returned[1][local], 0.0),
                jnp.where(later_inside, returned[2][local], 0.0),
            )
    reduced = own_rows(stack_states(running), slice_rows, pair_count)
    result_state = combine_states(reduced, stack_states(column_state))
    run_max, run_mass, run_sum = result_state
    my_counts = jnp.stack(
        [pick_entry(row_counts, block_of(own_index, local)) for local in range(local_blocks)]
    )
    row_valid = my_rows[None, :] < my_counts[:, None]
    near_sums = jnp.where(row_valid[..., None], run_sum / run_mass[..., None], 0.0).astype(
        jnp.bfloat16
    )
    log_masses = jnp.where(row_valid, run_max + jnp.log(run_mass), 0.0)
    return (near_sums, log_masses)


MESH = pl.DeviceIdType.MESH


def kernel(
    groups, blocks, rows, slice_rows, block_total,
    sizes_hbm, counts_hbm, emb_hbm, near_ref, mass_ref,
    sizes_ref, counts_ref, emb_ref, queries, keys, top, mass, total,
    chip_out, chip_in, chip_stats_out, chip_stats_in,
    pair_out, pair_in, pair_stats_out, pair_stats_in,
    load, share_send, share_recv, direct_send, key_recv, relay_send,
    chip_send, chip_recv, pair_send, pair_recv,
):
    width = emb_ref.shape[2]
    mine = lax.axis_index("own")
    half = lax.axis_index("pair")
    group, core = mine // 2, mine % 2
    toward = 1 - 2 * (group % 2)
    across = group + toward
    ahead, behind = group + 2 * toward, group - 2 * toward
    has_ahead = (ahead >= 0) & (ahead < groups)
    has_behind = (behind >= 0) & (behind < groups)
    behind2 = group - 4 * toward
    has_behind2 = (behind2 >= 0) & (behind2 < groups)
    slots = 2 * blocks
    half_rows = rows // 2
    core_rows = blocks * rows
    slot_keys = slots * slice_rows

    def device(group_index, core_index):
        return (group_index * 2 + core_index, half)

    partner = (mine, 1 - half)
    sibling = device(group, 1 - core)

    def half_span(side):
        return pl.ds(pl.multiple_of(side * half_rows, half_rows), half_rows)

    def load_rows(index, side):
        return pltpu.make_async_copy(
            emb_hbm.at[:, half_span(side)], emb_ref.at[:, half_span(side)], load.at[index]
        )

    load_rows(0, half).start()
    load_rows(1, 1 - half).start()
    load_sizes = pltpu.make_async_copy(sizes_hbm, sizes_ref, load.at[2])
    load_counts = pltpu.make_async_copy(counts_hbm, counts_ref, load.at[3])
    load_sizes.start()
    load_counts.start()

    barrier = pltpu.get_barrier_semaphore()

    def greet(target):
        pl.semaphore_signal(barrier, inc=1, device_id=target, device_id_type=MESH)

    greet(sibling)
    greet(partner)
    for other_core in range(2):
        greet(device(across, other_core))

    @pl.when(has_ahead)
    def _():
        for other_core in range(2):
            greet(device(ahead, other_core))

    @pl.when(has_behind)
    def _():
        for other_core in range(2):
            greet(device(behind, other_core))

    def normalise(side):
        for local in range(blocks):
            values = emb_ref[local, half_span(side), :]
            squares = jnp.sum(values * values, axis=-1, keepdims=True)
            queries[core * blocks + local, half_span(side), :] = (
                values * lax.rsqrt(squares + 1e-06)
            ).astype(jnp.bfloat16)

    load_rows(0, half).wait()
    normalise(half)

    own_blocks = pl.ds(core * blocks, blocks)
    other_blocks = pl.ds((1 - core) * blocks, blocks)

    def key_rows(core_index):
        return pl.ds(pl.multiple_of((half * 2 + core_index) * slice_rows, slice_rows), slice_rows)

    def share(index, side):
        return pltpu.make_async_remote_copy(
            src_ref=queries.at[own_blocks, half_span(side)],
            dst_ref=queries.at[own_blocks, half_span(side)],
            send_sem=share_send.at[index],
            recv_sem=share_recv.at[index],
            device_id=sibling,
            device_id_type=MESH,
        )

    def share_in(index, side):
        return pltpu.make_async_remote_copy(
            src_ref=queries.at[other_blocks, half_span(side)],
            dst_ref=queries.at[other_blocks, half_span(side)],
            send_sem=share_send.at[index],
            recv_sem=share_recv.at[index],
            device_id=sibling,
            device_id_type=MESH,
        )

    def direct(place, target, slot, other_core):
        return pltpu.make_async_remote_copy(
            src_ref=queries.at[own_blocks, key_rows(other_core)],
            dst_ref=keys.at[slot, core],
            send_sem=direct_send.at[place, other_core],
            recv_sem=key_recv.at[slot, core],
            device_id=device(target, other_core),
            device_id_type=MESH,
        )

    def relay(place, source, target, slot, part):
        return pltpu.make_async_remote_copy(
            src_ref=keys.at[source, part],
            dst_ref=keys.at[slot, part],
            send_sem=relay_send.at[place, part],
            recv_sem=key_recv.at[slot, part],
            device_id=device(target, core),
            device_id_type=MESH,
        )

    def arrived(slot, part):
        relay(0, slot, across, slot, part).wait_recv()

    def direct_across(other_core):
        return direct(0, across, 1, other_core)

    def direct_ahead(other_core):
        return direct(1, ahead, 3, other_core)

    def direct_behind(other_core):
        return direct(2, behind, 2, other_core)

    def relay_across(part):
        return relay(0, 2, across, 4, part)

    def relay_behind(part):
        return relay(1, 1, behind, 5, part)

    def relay_ahead(part):
        return relay(2, 4, ahead, 6, part)

    neighbours = 4 + 2 * has_ahead.astype(jnp.int32) + 2 * has_behind.astype(jnp.int32)
    pl.semaphore_wait(barrier, neighbours)

    for other_core in range(2):
        direct_across(other_core).start()

        @pl.when(has_behind)
        def _():
            direct_behind(other_core).start()

        @pl.when(has_ahead)
        def _():
            direct_ahead(other_core).start()

    share(0, half).start()
    load_rows(1, 1 - half).wait()
    normalise(1 - half)
    share(1, 1 - half).start()
    load_sizes.wait()
    load_counts.wait()

    starts = []
    so_far = jnp.int32(0)
    for cluster in range(sizes_ref.shape[0]):
        starts.append(so_far)
        so_far = so_far + sizes_ref[cluster]

    def cluster_of(ids):
        return sum((ids >= start).astype(jnp.int32) for start in starts)

    top[...] = jnp.full_like(top, negative)
    mass[...] = jnp.zeros_like(mass)
    total[...] = jnp.zeros_like(total)

    @pl.when(jnp.logical_not(has_ahead))
    def _():
        keys[2] = jnp.zeros_like(keys[2])
        keys[5] = jnp.zeros_like(keys[5])

    @pl.when(jnp.logical_not(has_behind))
    def _():
        keys[3] = jnp.zeros_like(keys[3])
        keys[4] = jnp.zeros_like(keys[4])

    @pl.when(jnp.logical_not(has_behind2))
    def _():
        keys[6] = jnp.zeros_like(keys[6])

    def fold(first_slot, distances, side_core):
        taken = len(distances)
        lane_ids = lax.broadcasted_iota(jnp.int32, (1, taken * slot_keys), 1)
        lane_local = lane_ids % slot_keys
        lane_row = lane_local % slice_rows + (half * 2 + core) * slice_rows
        lane_block = jnp.zeros_like(lane_ids)
        valid = jnp.zeros_like(lane_ids)
        for index, distance in enumerate(distances):
            first_block = (group + toward * distance) * slots
            for local in range(slots):
                block = first_block + local
                there = lane_ids // slice_rows == index * slots + local
                inside = (block >= 0) & (block < block_total)
                count = counts_ref[jnp.clip(block, 0, block_total - 1)]
                valid = jnp.where(there, jnp.where(inside, count, 0), valid)
                lane_block = jnp.where(there, block, lane_block)
        key_cluster = jnp.where(lane_row < valid, cluster_of(lane_block), -1)
        row_ids = lax.broadcasted_iota(jnp.int32, (core_rows, 1), 0) + (
            (group * 2 + side_core) * core_rows
        )
        query_cluster = cluster_of(row_ids // rows)
        block_keys = keys[first_slot:first_slot + taken] if isinstance(first_slot, int) else (
            keys[pl.ds(first_slot, taken)]
        )
        block_keys = block_keys.reshape(taken * slot_keys, width)
        side_blocks = pl.ds(side_core * blocks, blocks)
        span = pl.ds(pl.multiple_of(side_core * core_rows, core_rows), core_rows)
        scores = sharpness * lax.dot_general(
            queries[side_blocks].reshape(core_rows, width), block_keys,
            (((1,), (1,)), ((), ())), preferred_element_type=jnp.float32,
        )
        kept = query_cluster == key_cluster
        if taken == 1:
            kept = kept & (row_ids != lane_block * rows + lane_row)
        scores = jnp.where(kept, scores, 2.0 * negative)
        old_top = top[span]
        new_top = jnp.maximum(old_top, jnp.max(scores, axis=1, keepdims=True))
        scale = jnp.exp(old_top - new_top)
        weight = jnp.exp(scores - new_top)
        top[span] = new_top
        mass[span] = mass[span] * scale + jnp.sum(weight, axis=1, keepdims=True)
        weight = weight.astype(jnp.bfloat16)
        piece = min(256, width)
        for column in range(0, width, piece):
            columns = slice(column, column + piece)
            total[span, columns] = total[span, columns] * scale + jnp.dot(
                weight, block_keys[:, columns], preferred_element_type=jnp.float32
            )

    share_in(0, half).wait_recv()
    keys[0] = queries[:, key_rows(core), :].reshape(keys.shape[1:])
    share_in(1, 1 - half).wait_recv()

    def own_fold(side_core, carry):
        fold(0, (0,), side_core)
        return carry

    lax.fori_loop(0, 2, own_fold, 0)

    def pair_fold(turn, carry):
        @pl.when(turn == 0)
        def _():
            for part in range(2):
                arrived(1, part)

                @pl.when(has_behind)
                def _():
                    relay_behind(part).start()

            @pl.when(has_ahead)
            def _():
                for part in range(2):
                    arrived(2, part)
                    relay_across(part).start()

        @pl.when((turn == 2) & has_behind)
        def _():
            for part in range(2):
                arrived(4, part)

                @pl.when(has_ahead)
                def _():
                    relay_ahead(part).start()

            for part in range(2):
                arrived(3, part)

        late = turn // 2
        fold(1 + 2 * late, (1 - 3 * late, 2 - 3 * late), turn % 2)
        return carry

    lax.fori_loop(0, 4, pair_fold, 0)

    eye = (
        lax.broadcasted_iota(jnp.int32, (half_rows, half_rows), 0)
        == lax.broadcasted_iota(jnp.int32, (half_rows, half_rows), 1)
    )

    def to_lanes(column):
        return jnp.sum(jnp.where(eye, column, 0.0), axis=0, keepdims=True)

    def to_rows(lanes):
        return jnp.sum(jnp.where(eye, lanes, 0.0), axis=1, keepdims=True)

    def rows_of(block, side):
        return pl.ds(pl.multiple_of(block * rows + side * half_rows, half_rows), half_rows)

    def sent(source, target, send, recv, index, destination):
        return pltpu.make_async_remote_copy(
            src_ref=source, dst_ref=target, send_sem=send.at[index], recv_sem=recv.at[index],
            device_id=destination, device_id_type=MESH,
        )

    def chip_copy(remote):
        return sent(chip_out.at[remote], chip_in.at[remote], chip_send, chip_recv, remote, sibling)

    def pair_copy(local):
        return sent(pair_out.at[local], pair_in.at[local], pair_send, pair_recv, local, partner)

    chip_stats = sent(chip_stats_out, chip_stats_in, chip_send, chip_recv, 2, sibling)
    pair_stats = sent(pair_stats_out, pair_stats_in, pair_send, pair_recv, blocks, partner)
    sides = (1 - half, half)

    @pl.when(has_ahead)
    def _():
        for part in range(2):
            arrived(5, part)

    @pl.when(has_behind2)
    def _():
        for part in range(2):
            arrived(6, part)

    def last_fold(turn, carry):
        fold(5, (3, -3), jnp.where(turn == 0, 1 - core, core))

        @pl.when(turn == 0)
        def _():
            for remote in range(2):
                for local in range(blocks):
                    span = rows_of((1 - core) * blocks + local, sides[remote])
                    place = remote * blocks + local
                    chip_stats_out[place, 0:1, :half_rows] = to_lanes(top[span])
                    chip_stats_out[place, 1:2, :half_rows] = to_lanes(mass[span])
            chip_stats.start()
            for remote in range(2):
                for local in range(blocks):
                    span = rows_of((1 - core) * blocks + local, sides[remote])
                    chip_out[remote, local] = total[span].astype(jnp.bfloat16)
                chip_copy(remote).start()

        return carry

    lax.fori_loop(0, 2, last_fold, 0)

    chip_stats.wait_recv()
    scales = {}
    for remote in range(2):
        for local in range(blocks):
            span = rows_of(core * blocks + local, sides[remote])
            place = remote * blocks + local
            other_top = to_rows(chip_stats_in[place, 0:1, :half_rows])
            other_mass = to_rows(chip_stats_in[place, 1:2, :half_rows])
            new_top = jnp.maximum(top[span], other_top)
            scale = jnp.exp(top[span] - new_top)
            other_scale = jnp.exp(other_top - new_top)
            new_mass = mass[span] * scale + other_mass * other_scale
            scales[remote, local] = (scale, other_scale, new_top, new_mass)
            if remote == 0:
                pair_stats_out[local, 0:1, :half_rows] = to_lanes(new_top)
                pair_stats_out[local, 1:2, :half_rows] = to_lanes(new_mass)
    pair_stats.start()
    for remote in range(2):
        chip_copy(remote).wait_recv()
        for local in range(blocks):
            span = rows_of(core * blocks + local, sides[remote])
            scale, other_scale, new_top, new_mass = scales[remote, local]
            new_total = total[span] * scale + chip_in[remote, local].astype(jnp.float32) * other_scale
            if remote == 0:
                pair_out[local] = new_total.astype(jnp.bfloat16)
                pair_copy(local).start()
            else:
                total[span] = new_total

    place = lax.broadcasted_iota(jnp.int32, (half_rows, 1), 0) + half * half_rows
    pair_stats.wait_recv()
    final = []
    for local in range(blocks):
        other_top = to_rows(pair_stats_in[local, 0:1, :half_rows])
        other_mass = to_rows(pair_stats_in[local, 1:2, :half_rows])
        _, _, own_top, own_mass = scales[1, local]
        new_top = jnp.maximum(own_top, other_top)
        scale = jnp.exp(own_top - new_top)
        other_scale = jnp.exp(other_top - new_top)
        new_mass = own_mass * scale + other_mass * other_scale
        row_valid = place < counts_ref[mine * blocks + local]
        final.append((scale / new_mass, other_scale / new_mass, row_valid))
        logs = jnp.where(row_valid, new_top + jnp.log(new_mass), 0.0)
        mass_ref[local:local + 1, :] = to_lanes(logs)

    share(0, half).wait_send()
    share(1, 1 - half).wait_send()
    for other_core in range(2):
        direct_across(other_core).wait_send()

        @pl.when(has_ahead)
        def _():
            direct_ahead(other_core).wait_send()
            relay_across(other_core).wait_send()

        @pl.when(has_behind)
        def _():
            direct_behind(other_core).wait_send()
            relay_behind(other_core).wait_send()

        @pl.when(has_ahead & has_behind)
        def _():
            relay_ahead(other_core).wait_send()

    chip_stats.wait_send()
    pair_stats.wait_send()
    for remote in range(2):
        chip_copy(remote).wait_send()

    for local in range(blocks):
        pair_copy(local).wait_recv()
        span = rows_of(core * blocks + local, half)
        scale, other_scale, row_valid = final[local]
        merged = total[span] * scale + pair_in[local].astype(jnp.float32) * other_scale
        near_ref[local] = jnp.where(row_valid, merged, 0.0).astype(jnp.bfloat16)

    for local in range(blocks):
        pair_copy(local).wait_send()


def kernel_body(embeddings, cluster_sizes, row_counts):
    blocks, rows, width = embeddings.shape
    groups = lax.axis_size("own") // 2
    slots, slice_rows, half_rows = 2 * blocks, rows // 4, rows // 2
    query_rows = slots * rows
    wide, narrow = jnp.float32, jnp.bfloat16
    stats = (8, 128)
    dma = pltpu.SemaphoreType.DMA
    hbm, vmem = pl.BlockSpec(memory_space=pltpu.HBM), pl.BlockSpec(memory_space=pltpu.VMEM)
    return pl.pallas_call(
        functools.partial(kernel, groups, blocks, rows, slice_rows, row_counts.shape[0]),
        out_shape=(
            jax.ShapeDtypeStruct((blocks, half_rows, width), narrow),
            jax.ShapeDtypeStruct((blocks, half_rows), wide),
        ),
        in_specs=[hbm, hbm, hbm],
        out_specs=(vmem, vmem),
        scratch_shapes=[
            pltpu.SMEM(cluster_sizes.shape, jnp.int32),
            pltpu.SMEM(row_counts.shape, jnp.int32),
            pltpu.VMEM(embeddings.shape, wide),
            pltpu.VMEM((slots, rows, width), narrow),
            pltpu.VMEM((7, 2, blocks, slice_rows, width), narrow),
            pltpu.VMEM((query_rows, 1), wide),
            pltpu.VMEM((query_rows, 1), wide),
            pltpu.VMEM((query_rows, width), wide),
            pltpu.VMEM((2, blocks, half_rows, width), narrow),
            pltpu.VMEM((2, blocks, half_rows, width), narrow),
            pltpu.VMEM((2 * blocks, *stats), wide),
            pltpu.VMEM((2 * blocks, *stats), wide),
            pltpu.VMEM((blocks, half_rows, width), narrow),
            pltpu.VMEM((blocks, half_rows, width), narrow),
            pltpu.VMEM((blocks, *stats), wide),
            pltpu.VMEM((blocks, *stats), wide),
            dma((4,)), dma((2,)), dma((2,)),
            dma((3, 2)), dma((7, 2)), dma((3, 2)),
            dma((3,)), dma((3,)), dma((blocks + 1,)), dma((blocks + 1,)),
        ],
        compiler_params=pltpu.CompilerParams(
            collective_id=0, has_side_effects=True, vmem_limit_bytes=56 * 1024 * 1024
        ),
        cost_estimate=pl.CostEstimate(
            flops=4 * query_rows * 7 * slots * slice_rows * width,
            bytes_accessed=embeddings.size * 4,
            transcendentals=query_rows * 7 * slots * slice_rows,
        ),
    )(cluster_sizes, row_counts, embeddings)


def fits_kernel(block_shape):
    blocks, rows, width = block_shape
    covered = (SPAN + 2 * blocks - 2) // (2 * blocks) <= 3
    whole_tiles = rows % 128 == 0 and width % 128 == 0
    return lax.axis_size("pair") == 2 and lax.axis_size("own") % 4 == 0 and covered and whole_tiles


def device_part(embeddings, cluster_sizes, row_counts):
    chosen = kernel_body if fits_kernel(embeddings.shape) else body
    return chosen(embeddings, cluster_sizes, row_counts)


def solution(mesh):
    placed = (P("own", None, None), P(), P())
    return jax.shard_map(
        device_part,
        mesh=mesh,
        in_specs=placed,
        out_specs=(P("own", "pair", None), P("own", "pair")),
        check_vma=False,
    )
```

```python
import functools

import jax
import jax.numpy as jnp
from jax import lax
from jax.experimental import pallas as pl
from jax.experimental.pallas import tpu as pltpu
from jax.sharding import PartitionSpec as P

SPAN = 12


sharpness = 128.0
negative = -1e30


def passed_along(shard, axis, by):
    count = lax.axis_size(axis)
    pairs = [(i, i + by) for i in range(count) if 0 <= i + by < count]
    return lax.ppermute(shard, axis, pairs)


def unit_rows(values):
    squares = jnp.sum(values * values, axis=-1, keepdims=True)
    return (values * lax.rsqrt(squares + 1e-06)).astype(jnp.bfloat16)


def fold_in(running, row_top, row_total, partial_value):
    run_max, run_mass, run_sum = running
    new_max = jnp.maximum(run_max, row_top)
    old_scale = jnp.exp(run_max - new_max)
    new_scale = jnp.exp(row_top - new_max)
    return (
        new_max,
        run_mass * old_scale + row_total * new_scale,
        run_sum * old_scale[..., None] + partial_value * new_scale[..., None],
    )


def combine_states(first_state, second_state):
    return fold_in(first_state, second_state[0], second_state[1], second_state[2])


def row_stats(scores, kept, key_rows):
    scores = jnp.where(kept, scores, negative)
    row_top = jnp.max(scores, axis=1)
    weight = jnp.where(kept, jnp.exp(scores - row_top[:, None]), 0.0)
    partial_value = jnp.dot(
        weight.astype(jnp.bfloat16), key_rows, preferred_element_type=jnp.float32
    )
    return (row_top, jnp.sum(weight, axis=1), partial_value)


def pick_entry(table, position):
    places = jnp.arange(table.shape[0], dtype=jnp.int32)
    return jnp.sum(jnp.where(places == position, table, 0))


def empty_state(row_total, feature_count):
    return (
        jnp.full((row_total,), negative, jnp.float32),
        jnp.zeros((row_total,), jnp.float32),
        jnp.zeros((row_total, feature_count), jnp.float32),
    )


def stack_states(states):
    return tuple((jnp.stack([state[field] for state in states]) for field in range(3)))


def own_rows(stacked, slice_rows, pair_count):
    run_max, run_mass, run_sum = stacked
    local_blocks = run_max.shape[0]
    feature_count = run_sum.shape[2]
    arrived = (
        lax.all_to_all(
            run_max.reshape(local_blocks, pair_count, slice_rows),
            "pair",
            split_axis=1,
            concat_axis=1,
            tiled=True,
        ),
        lax.all_to_all(
            run_mass.reshape(local_blocks, pair_count, slice_rows),
            "pair",
            split_axis=1,
            concat_axis=1,
            tiled=True,
        ),
        lax.all_to_all(
            run_sum.reshape(local_blocks, pair_count, slice_rows, feature_count),
            "pair",
            split_axis=1,
            concat_axis=1,
            tiled=True,
        ),
    )
    new_max = jnp.max(arrived[0], axis=1)
    scales = jnp.exp(arrived[0] - new_max[:, None, :])
    return (
        new_max,
        jnp.sum(arrived[1] * scales, axis=1),
        jnp.sum(arrived[2] * scales[..., None], axis=1),
    )


def body(embeddings, cluster_sizes, row_counts):
    normed = unit_rows(embeddings)
    local_blocks, block_rows, feature_count = normed.shape
    pair_count = lax.axis_size("pair")
    own_count = lax.axis_size("own")
    block_total = own_count * local_blocks
    slice_rows = block_rows // pair_count
    own_index = lax.axis_index("own")
    slice_start = lax.axis_index("pair") * slice_rows
    my_slice = lax.dynamic_slice_in_dim(normed, slice_start, slice_rows, 1)
    cluster_start = jnp.cumsum(cluster_sizes) - cluster_sizes
    block_ids = jnp.arange(block_total, dtype=jnp.int32)
    owner_cluster = (
        jnp.sum((block_ids[:, None] >= cluster_start[None, :]).astype(jnp.int32), axis=1) - 1
    )
    full_rows = jnp.arange(block_rows, dtype=jnp.int32)
    my_rows = slice_start + jnp.arange(slice_rows, dtype=jnp.int32)
    offset_count = (SPAN + local_blocks - 2) // local_blocks

    def block_of(owner, local):
        return owner * local_blocks + local

    def linked_to(query_block, source):
        inside = (source >= 0) & (source < block_total)
        return inside & (
            pick_entry(owner_cluster, source) == pick_entry(owner_cluster, query_block)
        )

    def key_mask(query_block, source):
        valid_keys = my_rows[None, :] < pick_entry(row_counts, source)
        not_self = (query_block != source) | (full_rows[:, None] != my_rows[None, :])
        return linked_to(query_block, source) & valid_keys & not_self

    def tile_scores(queries, key_rows):
        return sharpness * jnp.dot(queries, key_rows.T, preferred_element_type=jnp.float32)

    running = [empty_state(block_rows, feature_count) for local in range(local_blocks)]
    for local in range(local_blocks):
        query_block = block_of(own_index, local)
        for other in range(local_blocks):
            source = block_of(own_index, other)
            row_top, row_total, partial_value = row_stats(
                tile_scores(normed[local], my_slice[other]),
                key_mask(query_block, source),
                my_slice[other],
            )
            running[local] = fold_in(running[local], row_top, row_total, partial_value)
    column_state = [empty_state(slice_rows, feature_count) for local in range(local_blocks)]
    for offset in range(1, offset_count + 1):
        earlier = passed_along(my_slice, "own", offset)
        back_states = [empty_state(slice_rows, feature_count) for local in range(local_blocks)]
        for local in range(local_blocks):
            query_block = block_of(own_index, local)
            query_valid = full_rows < pick_entry(row_counts, query_block)
            for other in range(local_blocks):
                source = block_of(own_index - offset, other)
                scores = tile_scores(normed[local], earlier[other])
                row_top, row_total, partial_value = row_stats(
                    scores, key_mask(query_block, source), earlier[other]
                )
                running[local] = fold_in(running[local], row_top, row_total, partial_value)
                back_mask = (
                    linked_to(query_block, source) & query_valid[None, :] & (my_rows[:, None] >= 0)
                )
                back_top, back_total, back_sum = row_stats(scores.T, back_mask, normed[local])
                back_states[other] = fold_in(back_states[other], back_top, back_total, back_sum)
        stacked_back = stack_states(back_states)
        returned = passed_along((stacked_back[0], stacked_back[1], stacked_back[2]), "own", -offset)
        later_inside = own_index + offset < own_count
        for local in range(local_blocks):
            column_state[local] = fold_in(
                column_state[local],
                jnp.where(later_inside, returned[0][local], negative),
                jnp.where(later_inside, returned[1][local], 0.0),
                jnp.where(later_inside, returned[2][local], 0.0),
            )
    reduced = own_rows(stack_states(running), slice_rows, pair_count)
    result_state = combine_states(reduced, stack_states(column_state))
    run_max, run_mass, run_sum = result_state
    my_counts = jnp.stack(
        [pick_entry(row_counts, block_of(own_index, local)) for local in range(local_blocks)]
    )
    row_valid = my_rows[None, :] < my_counts[:, None]
    near_sums = jnp.where(row_valid[..., None], run_sum / run_mass[..., None], 0.0).astype(
        jnp.bfloat16
    )
    log_masses = jnp.where(row_valid, run_max + jnp.log(run_mass), 0.0)
    return (near_sums, log_masses)


MESH = pl.DeviceIdType.MESH


def kernel(
    groups, blocks, rows, slice_rows, block_total,
    sizes_hbm, counts_hbm, emb_hbm, near_ref, mass_ref,
    sizes_ref, counts_ref, emb_ref, queries, keys, top, mass, total,
    chip_out, chip_in, chip_stats_out, chip_stats_in,
    pair_out, pair_in, pair_stats_out, pair_stats_in,
    load, share_send, share_recv, direct_send, key_recv, relay_send,
    chip_send, chip_recv, pair_send, pair_recv,
):
    width = emb_ref.shape[2]
    mine = lax.axis_index("own")
    half = lax.axis_index("pair")
    group, core = mine // 2, mine % 2
    toward = 1 - 2 * (group % 2)
    across = group + toward
    ahead, behind = group + 2 * toward, group - 2 * toward
    has_ahead = (ahead >= 0) & (ahead < groups)
    has_behind = (behind >= 0) & (behind < groups)
    behind2 = group - 4 * toward
    has_behind2 = (behind2 >= 0) & (behind2 < groups)
    slots = 2 * blocks
    half_rows = rows // 2
    core_rows = blocks * rows
    slot_keys = slots * slice_rows

    def device(group_index, core_index):
        return (group_index * 2 + core_index, half)

    partner = (mine, 1 - half)
    sibling = device(group, 1 - core)

    def half_span(side):
        return pl.ds(pl.multiple_of(side * half_rows, half_rows), half_rows)

    def load_rows(index, side):
        return pltpu.make_async_copy(
            emb_hbm.at[:, half_span(side)], emb_ref.at[:, half_span(side)], load.at[index]
        )

    load_rows(0, half).start()
    load_rows(1, 1 - half).start()
    load_sizes = pltpu.make_async_copy(sizes_hbm, sizes_ref, load.at[2])
    load_counts = pltpu.make_async_copy(counts_hbm, counts_ref, load.at[3])
    load_sizes.start()
    load_counts.start()

    barrier = pltpu.get_barrier_semaphore()

    def greet(target):
        pl.semaphore_signal(barrier, inc=1, device_id=target, device_id_type=MESH)

    greet(sibling)
    greet(partner)
    for other_core in range(2):
        greet(device(across, other_core))

    @pl.when(has_ahead)
    def _():
        for other_core in range(2):
            greet(device(ahead, other_core))

    @pl.when(has_behind)
    def _():
        for other_core in range(2):
            greet(device(behind, other_core))

    def normalise(side):
        for local in range(blocks):
            values = emb_ref[local, half_span(side), :]
            squares = jnp.sum(values * values, axis=-1, keepdims=True)
            queries[core * blocks + local, half_span(side), :] = (
                values * lax.rsqrt(squares + 1e-06)
            ).astype(jnp.bfloat16)

    load_rows(0, half).wait()
    normalise(half)

    own_blocks = pl.ds(core * blocks, blocks)
    other_blocks = pl.ds((1 - core) * blocks, blocks)

    def key_rows(core_index):
        return pl.ds(pl.multiple_of((half * 2 + core_index) * slice_rows, slice_rows), slice_rows)

    def share(index, side):
        return pltpu.make_async_remote_copy(
            src_ref=queries.at[own_blocks, half_span(side)],
            dst_ref=queries.at[own_blocks, half_span(side)],
            send_sem=share_send.at[index],
            recv_sem=share_recv.at[index],
            device_id=sibling,
            device_id_type=MESH,
        )

    def share_in(index, side):
        return pltpu.make_async_remote_copy(
            src_ref=queries.at[other_blocks, half_span(side)],
            dst_ref=queries.at[other_blocks, half_span(side)],
            send_sem=share_send.at[index],
            recv_sem=share_recv.at[index],
            device_id=sibling,
            device_id_type=MESH,
        )

    def direct(place, target, slot, other_core, local):
        block = core * blocks + local
        return pltpu.make_async_remote_copy(
            src_ref=queries.at[block, key_rows(other_core)],
            dst_ref=keys.at[slot, block],
            send_sem=direct_send.at[place, other_core, local],
            recv_sem=key_recv.at[slot, block],
            device_id=device(target, other_core),
            device_id_type=MESH,
        )

    def relay(place, source, target, slot, block):
        return pltpu.make_async_remote_copy(
            src_ref=keys.at[source, block],
            dst_ref=keys.at[slot, block],
            send_sem=relay_send.at[place, block],
            recv_sem=key_recv.at[slot, block],
            device_id=device(target, core),
            device_id_type=MESH,
        )

    def arrived(slot, block):
        relay(0, slot, across, slot, block).wait_recv()

    def direct_across(other_core, local):
        return direct(0, across, 1, other_core, local)

    def direct_ahead(other_core, local):
        return direct(1, ahead, 3, other_core, local)

    def direct_behind(other_core, local):
        return direct(2, behind, 2, other_core, local)

    skip = (1 - toward) // 2
    reach = slots - 1

    def upper(index):
        return index + 1 - skip

    def lower(index):
        return index + skip

    def relay_across(index):
        return relay(0, 2, across, 4, (index + skip) % slots)

    def relay_behind(index):
        return relay(1, 1, behind, 5, lower(index))

    def relay_ahead(index):
        return relay(2, 4, ahead, 6, upper(index))

    neighbours = 4 + 2 * has_ahead.astype(jnp.int32) + 2 * has_behind.astype(jnp.int32)
    pl.semaphore_wait(barrier, neighbours)

    for other_core in range(2):
        for local in range(blocks):
            direct_across(other_core, local).start()

            @pl.when(has_behind)
            def _():
                direct_behind(other_core, local).start()

            @pl.when(has_ahead)
            def _():
                direct_ahead(other_core, local).start()

    share(0, half).start()
    load_rows(1, 1 - half).wait()
    normalise(1 - half)
    share(1, 1 - half).start()
    load_sizes.wait()
    load_counts.wait()

    starts = []
    so_far = jnp.int32(0)
    for cluster in range(sizes_ref.shape[0]):
        starts.append(so_far)
        so_far = so_far + sizes_ref[cluster]

    def cluster_of(ids):
        return sum((ids >= start).astype(jnp.int32) for start in starts)

    top[...] = jnp.full_like(top, negative)
    mass[...] = jnp.zeros_like(mass)
    total[...] = jnp.zeros_like(total)

    @pl.when(jnp.logical_not(has_ahead))
    def _():
        keys[2] = jnp.zeros_like(keys[2])
        keys[5] = jnp.zeros_like(keys[5])

    @pl.when(jnp.logical_not(has_behind))
    def _():
        keys[3] = jnp.zeros_like(keys[3])
        keys[4] = jnp.zeros_like(keys[4])

    @pl.when(has_ahead)
    def _():
        keys[5, lower(reach) % slots] = jnp.zeros_like(keys[5, 0])

    @pl.when(has_behind2)
    def _():
        keys[6, upper(reach) % slots] = jnp.zeros_like(keys[6, 0])

    @pl.when(jnp.logical_not(has_behind2))
    def _():
        keys[6] = jnp.zeros_like(keys[6])

    own_slot = 0

    def fold(first_slot, distances, side_core):
        taken = len(distances)
        lane_ids = lax.broadcasted_iota(jnp.int32, (1, taken * slot_keys), 1)
        lane_local = lane_ids % slot_keys
        lane_row = lane_local % slice_rows + (half * 2 + core) * slice_rows
        lane_block = jnp.zeros_like(lane_ids)
        valid = jnp.zeros_like(lane_ids)
        for index, distance in enumerate(distances):
            first_block = (group + toward * distance) * slots
            for local in range(slots):
                block = first_block + local
                there = lane_ids // slice_rows == index * slots + local
                inside = (block >= 0) & (block < block_total)
                count = counts_ref[jnp.clip(block, 0, block_total - 1)]
                valid = jnp.where(there, jnp.where(inside, count, 0), valid)
                lane_block = jnp.where(there, block, lane_block)
        key_cluster = jnp.where(lane_row < valid, cluster_of(lane_block), -1)
        row_ids = lax.broadcasted_iota(jnp.int32, (core_rows, 1), 0) + (
            (group * 2 + side_core) * core_rows
        )
        query_cluster = cluster_of(row_ids // rows)
        block_keys = keys[first_slot:first_slot + taken] if isinstance(first_slot, int) else (
            keys[pl.ds(first_slot, taken)]
        )
        block_keys = block_keys.reshape(taken * slot_keys, width)
        side_blocks = pl.ds(side_core * blocks, blocks)
        span = pl.ds(pl.multiple_of(side_core * core_rows, core_rows), core_rows)
        scores = sharpness * lax.dot_general(
            queries[side_blocks].reshape(core_rows, width), block_keys,
            (((1,), (1,)), ((), ())), preferred_element_type=jnp.float32,
        )
        kept = query_cluster == key_cluster
        if first_slot is own_slot:
            kept = kept & (row_ids != lane_block * rows + lane_row)
        scores = jnp.where(kept, scores, 2.0 * negative)
        old_top = top[span]
        new_top = jnp.maximum(old_top, jnp.max(scores, axis=1, keepdims=True))
        scale = jnp.exp(old_top - new_top)
        weight = jnp.exp(scores - new_top)
        top[span] = new_top
        mass[span] = mass[span] * scale + jnp.sum(weight, axis=1, keepdims=True)
        weight = weight.astype(jnp.bfloat16)
        piece = min(256, width)
        for column in range(0, width, piece):
            columns = slice(column, column + piece)
            total[span, columns] = total[span, columns] * scale + jnp.dot(
                weight, block_keys[:, columns], preferred_element_type=jnp.float32
            )

    share_in(0, half).wait_recv()
    keys[0] = queries[:, key_rows(core), :]
    share_in(1, 1 - half).wait_recv()

    def own_fold(side_core, carry):
        fold(own_slot, (0,), side_core)
        return carry

    lax.fori_loop(0, 2, own_fold, 0)

    def pair_fold(turn, carry):
        @pl.when(turn == 0)
        def _():
            @pl.when(has_ahead)
            def _():
                for index in range(slots):
                    arrived(2, (index + skip) % slots)
                    relay_across(index).start()

            for index in range(reach):
                arrived(1, lower(index))

                @pl.when(has_behind)
                def _():
                    relay_behind(index).start()

            arrived(1, lower(reach) % slots)

        @pl.when((turn == 2) & has_behind)
        def _():
            for index in range(reach):
                arrived(4, upper(index))

                @pl.when(has_ahead)
                def _():
                    relay_ahead(index).start()

            arrived(4, upper(reach) % slots)
            for block in range(slots):
                arrived(3, block)

        late = turn // 2
        fold(1 + 2 * late, (1 - 3 * late, 2 - 3 * late), turn % 2)
        return carry

    lax.fori_loop(0, 4, pair_fold, 0)

    eye = (
        lax.broadcasted_iota(jnp.int32, (half_rows, half_rows), 0)
        == lax.broadcasted_iota(jnp.int32, (half_rows, half_rows), 1)
    )

    def to_lanes(column):
        return jnp.sum(jnp.where(eye, column, 0.0), axis=0, keepdims=True)

    def to_rows(lanes):
        return jnp.sum(jnp.where(eye, lanes, 0.0), axis=1, keepdims=True)

    def rows_of(block, side):
        return pl.ds(pl.multiple_of(block * rows + side * half_rows, half_rows), half_rows)

    def sent(source, target, send, recv, index, destination):
        return pltpu.make_async_remote_copy(
            src_ref=source, dst_ref=target, send_sem=send.at[index], recv_sem=recv.at[index],
            device_id=destination, device_id_type=MESH,
        )

    def chip_copy(remote):
        return sent(chip_out.at[remote], chip_in.at[remote], chip_send, chip_recv, remote, sibling)

    def pair_copy(local):
        return sent(pair_out.at[local], pair_in.at[local], pair_send, pair_recv, local, partner)

    chip_stats = sent(chip_stats_out, chip_stats_in, chip_send, chip_recv, 2, sibling)
    pair_stats = sent(pair_stats_out, pair_stats_in, pair_send, pair_recv, blocks, partner)
    sides = (1 - half, half)

    @pl.when(has_ahead)
    def _():
        for index in range(reach):
            arrived(5, lower(index))

    def late_fold(side_core, carry):
        fold(5, (3,), side_core)
        return carry

    lax.fori_loop(0, 2, late_fold, 0)

    @pl.when(has_behind2)
    def _():
        for index in range(reach):
            arrived(6, upper(index))

    def last_fold(turn, carry):
        fold(6, (-3,), jnp.where(turn == 0, 1 - core, core))

        @pl.when(turn == 0)
        def _():
            for remote in range(2):
                for local in range(blocks):
                    span = rows_of((1 - core) * blocks + local, sides[remote])
                    place = remote * blocks + local
                    chip_stats_out[place, 0:1, :half_rows] = to_lanes(top[span])
                    chip_stats_out[place, 1:2, :half_rows] = to_lanes(mass[span])
            chip_stats.start()
            for remote in range(2):
                for local in range(blocks):
                    span = rows_of((1 - core) * blocks + local, sides[remote])
                    chip_out[remote, local] = total[span].astype(jnp.bfloat16)
                chip_copy(remote).start()

        return carry

    lax.fori_loop(0, 2, last_fold, 0)

    chip_stats.wait_recv()
    scales = {}
    for remote in range(2):
        for local in range(blocks):
            span = rows_of(core * blocks + local, sides[remote])
            place = remote * blocks + local
            other_top = to_rows(chip_stats_in[place, 0:1, :half_rows])
            other_mass = to_rows(chip_stats_in[place, 1:2, :half_rows])
            new_top = jnp.maximum(top[span], other_top)
            scale = jnp.exp(top[span] - new_top)
            other_scale = jnp.exp(other_top - new_top)
            new_mass = mass[span] * scale + other_mass * other_scale
            scales[remote, local] = (scale, other_scale, new_top, new_mass)
            if remote == 0:
                pair_stats_out[local, 0:1, :half_rows] = to_lanes(new_top)
                pair_stats_out[local, 1:2, :half_rows] = to_lanes(new_mass)
    pair_stats.start()
    for remote in range(2):
        chip_copy(remote).wait_recv()
        for local in range(blocks):
            span = rows_of(core * blocks + local, sides[remote])
            scale, other_scale, new_top, new_mass = scales[remote, local]
            new_total = total[span] * scale + chip_in[remote, local].astype(jnp.float32) * other_scale
            if remote == 0:
                pair_out[local] = new_total.astype(jnp.bfloat16)
                pair_copy(local).start()
            else:
                total[span] = new_total

    place = lax.broadcasted_iota(jnp.int32, (half_rows, 1), 0) + half * half_rows
    pair_stats.wait_recv()
    final = []
    for local in range(blocks):
        other_top = to_rows(pair_stats_in[local, 0:1, :half_rows])
        other_mass = to_rows(pair_stats_in[local, 1:2, :half_rows])
        _, _, own_top, own_mass = scales[1, local]
        new_top = jnp.maximum(own_top, other_top)
        scale = jnp.exp(own_top - new_top)
        other_scale = jnp.exp(other_top - new_top)
        new_mass = own_mass * scale + other_mass * other_scale
        row_valid = place < counts_ref[mine * blocks + local]
        final.append((scale / new_mass, other_scale / new_mass, row_valid))
        logs = jnp.where(row_valid, new_top + jnp.log(new_mass), 0.0)
        mass_ref[local:local + 1, :] = to_lanes(logs)

    share(0, half).wait_send()
    share(1, 1 - half).wait_send()
    for other_core in range(2):
        for local in range(blocks):
            direct_across(other_core, local).wait_send()

            @pl.when(has_ahead)
            def _():
                direct_ahead(other_core, local).wait_send()

            @pl.when(has_behind)
            def _():
                direct_behind(other_core, local).wait_send()

    @pl.when(has_ahead)
    def _():
        for index in range(slots):
            relay_across(index).wait_send()

    @pl.when(has_behind)
    def _():
        for index in range(reach):
            relay_behind(index).wait_send()

    @pl.when(has_ahead & has_behind)
    def _():
        for index in range(reach):
            relay_ahead(index).wait_send()

    chip_stats.wait_send()
    pair_stats.wait_send()
    for remote in range(2):
        chip_copy(remote).wait_send()

    for local in range(blocks):
        pair_copy(local).wait_recv()
        span = rows_of(core * blocks + local, half)
        scale, other_scale, row_valid = final[local]
        merged = total[span] * scale + pair_in[local].astype(jnp.float32) * other_scale
        near_ref[local] = jnp.where(row_valid, merged, 0.0).astype(jnp.bfloat16)

    for local in range(blocks):
        pair_copy(local).wait_send()


def kernel_body(embeddings, cluster_sizes, row_counts):
    blocks, rows, width = embeddings.shape
    groups = lax.axis_size("own") // 2
    slots, slice_rows, half_rows = 2 * blocks, rows // 4, rows // 2
    query_rows = slots * rows
    wide, narrow = jnp.float32, jnp.bfloat16
    stats = (8, 128)
    dma = pltpu.SemaphoreType.DMA
    hbm, vmem = pl.BlockSpec(memory_space=pltpu.HBM), pl.BlockSpec(memory_space=pltpu.VMEM)
    return pl.pallas_call(
        functools.partial(kernel, groups, blocks, rows, slice_rows, row_counts.shape[0]),
        out_shape=(
            jax.ShapeDtypeStruct((blocks, half_rows, width), narrow),
            jax.ShapeDtypeStruct((blocks, half_rows), wide),
        ),
        in_specs=[hbm, hbm, hbm],
        out_specs=(vmem, vmem),
        scratch_shapes=[
            pltpu.SMEM(cluster_sizes.shape, jnp.int32),
            pltpu.SMEM(row_counts.shape, jnp.int32),
            pltpu.VMEM(embeddings.shape, wide),
            pltpu.VMEM((slots, rows, width), narrow),
            pltpu.VMEM((7, slots, slice_rows, width), narrow),
            pltpu.VMEM((query_rows, 1), wide),
            pltpu.VMEM((query_rows, 1), wide),
            pltpu.VMEM((query_rows, width), wide),
            pltpu.VMEM((2, blocks, half_rows, width), narrow),
            pltpu.VMEM((2, blocks, half_rows, width), narrow),
            pltpu.VMEM((2 * blocks, *stats), wide),
            pltpu.VMEM((2 * blocks, *stats), wide),
            pltpu.VMEM((blocks, half_rows, width), narrow),
            pltpu.VMEM((blocks, half_rows, width), narrow),
            pltpu.VMEM((blocks, *stats), wide),
            pltpu.VMEM((blocks, *stats), wide),
            dma((4,)), dma((2,)), dma((2,)),
            dma((3, 2, blocks)), dma((7, slots)), dma((3, slots)),
            dma((3,)), dma((3,)), dma((blocks + 1,)), dma((blocks + 1,)),
        ],
        compiler_params=pltpu.CompilerParams(
            collective_id=0, has_side_effects=True, vmem_limit_bytes=56 * 1024 * 1024
        ),
        cost_estimate=pl.CostEstimate(
            flops=4 * query_rows * 7 * slots * slice_rows * width,
            bytes_accessed=embeddings.size * 4,
            transcendentals=query_rows * 7 * slots * slice_rows,
        ),
    )(cluster_sizes, row_counts, embeddings)


def fits_kernel(block_shape):
    blocks, rows, width = block_shape
    covered = (SPAN + 2 * blocks - 2) // (2 * blocks) <= 3
    far_enough = 3 * 2 * blocks >= SPAN
    whole_tiles = rows % 128 == 0 and width % 128 == 0
    return lax.axis_size("pair") == 2 and lax.axis_size("own") % 4 == 0 and (
        covered and far_enough and whole_tiles
    )


def device_part(embeddings, cluster_sizes, row_counts):
    chosen = kernel_body if fits_kernel(embeddings.shape) else body
    return chosen(embeddings, cluster_sizes, row_counts)


def solution(mesh):
    placed = (P("own", None, None), P(), P())
    return jax.shard_map(
        device_part,
        mesh=mesh,
        in_specs=placed,
        out_specs=(P("own", "pair", None), P("own", "pair")),
        check_vma=False,
    )
```

```python
import functools

import jax
import jax.numpy as jnp
from jax import lax
from jax.experimental import pallas as pl
from jax.experimental.pallas import tpu as pltpu
from jax.sharding import PartitionSpec as P

SPAN = 12


sharpness = 128.0
negative = -1e30


def passed_along(shard, axis, by):
    count = lax.axis_size(axis)
    pairs = [(i, i + by) for i in range(count) if 0 <= i + by < count]
    return lax.ppermute(shard, axis, pairs)


def unit_rows(values):
    squares = jnp.sum(values * values, axis=-1, keepdims=True)
    return (values * lax.rsqrt(squares + 1e-06)).astype(jnp.bfloat16)


def fold_in(running, row_top, row_total, partial_value):
    run_max, run_mass, run_sum = running
    new_max = jnp.maximum(run_max, row_top)
    old_scale = jnp.exp(run_max - new_max)
    new_scale = jnp.exp(row_top - new_max)
    return (
        new_max,
        run_mass * old_scale + row_total * new_scale,
        run_sum * old_scale[..., None] + partial_value * new_scale[..., None],
    )


def combine_states(first_state, second_state):
    return fold_in(first_state, second_state[0], second_state[1], second_state[2])


def row_stats(scores, kept, key_rows):
    scores = jnp.where(kept, scores, negative)
    row_top = jnp.max(scores, axis=1)
    weight = jnp.where(kept, jnp.exp(scores - row_top[:, None]), 0.0)
    partial_value = jnp.dot(
        weight.astype(jnp.bfloat16), key_rows, preferred_element_type=jnp.float32
    )
    return (row_top, jnp.sum(weight, axis=1), partial_value)


def pick_entry(table, position):
    places = jnp.arange(table.shape[0], dtype=jnp.int32)
    return jnp.sum(jnp.where(places == position, table, 0))


def empty_state(row_total, feature_count):
    return (
        jnp.full((row_total,), negative, jnp.float32),
        jnp.zeros((row_total,), jnp.float32),
        jnp.zeros((row_total, feature_count), jnp.float32),
    )


def stack_states(states):
    return tuple((jnp.stack([state[field] for state in states]) for field in range(3)))


def own_rows(stacked, slice_rows, pair_count):
    run_max, run_mass, run_sum = stacked
    local_blocks = run_max.shape[0]
    feature_count = run_sum.shape[2]
    arrived = (
        lax.all_to_all(
            run_max.reshape(local_blocks, pair_count, slice_rows),
            "pair",
            split_axis=1,
            concat_axis=1,
            tiled=True,
        ),
        lax.all_to_all(
            run_mass.reshape(local_blocks, pair_count, slice_rows),
            "pair",
            split_axis=1,
            concat_axis=1,
            tiled=True,
        ),
        lax.all_to_all(
            run_sum.reshape(local_blocks, pair_count, slice_rows, feature_count),
            "pair",
            split_axis=1,
            concat_axis=1,
            tiled=True,
        ),
    )
    new_max = jnp.max(arrived[0], axis=1)
    scales = jnp.exp(arrived[0] - new_max[:, None, :])
    return (
        new_max,
        jnp.sum(arrived[1] * scales, axis=1),
        jnp.sum(arrived[2] * scales[..., None], axis=1),
    )


def body(embeddings, cluster_sizes, row_counts):
    normed = unit_rows(embeddings)
    local_blocks, block_rows, feature_count = normed.shape
    pair_count = lax.axis_size("pair")
    own_count = lax.axis_size("own")
    block_total = own_count * local_blocks
    slice_rows = block_rows // pair_count
    own_index = lax.axis_index("own")
    slice_start = lax.axis_index("pair") * slice_rows
    my_slice = lax.dynamic_slice_in_dim(normed, slice_start, slice_rows, 1)
    cluster_start = jnp.cumsum(cluster_sizes) - cluster_sizes
    block_ids = jnp.arange(block_total, dtype=jnp.int32)
    owner_cluster = (
        jnp.sum((block_ids[:, None] >= cluster_start[None, :]).astype(jnp.int32), axis=1) - 1
    )
    full_rows = jnp.arange(block_rows, dtype=jnp.int32)
    my_rows = slice_start + jnp.arange(slice_rows, dtype=jnp.int32)
    offset_count = (SPAN + local_blocks - 2) // local_blocks

    def block_of(owner, local):
        return owner * local_blocks + local

    def linked_to(query_block, source):
        inside = (source >= 0) & (source < block_total)
        return inside & (
            pick_entry(owner_cluster, source) == pick_entry(owner_cluster, query_block)
        )

    def key_mask(query_block, source):
        valid_keys = my_rows[None, :] < pick_entry(row_counts, source)
        not_self = (query_block != source) | (full_rows[:, None] != my_rows[None, :])
        return linked_to(query_block, source) & valid_keys & not_self

    def tile_scores(queries, key_rows):
        return sharpness * jnp.dot(queries, key_rows.T, preferred_element_type=jnp.float32)

    running = [empty_state(block_rows, feature_count) for local in range(local_blocks)]
    for local in range(local_blocks):
        query_block = block_of(own_index, local)
        for other in range(local_blocks):
            source = block_of(own_index, other)
            row_top, row_total, partial_value = row_stats(
                tile_scores(normed[local], my_slice[other]),
                key_mask(query_block, source),
                my_slice[other],
            )
            running[local] = fold_in(running[local], row_top, row_total, partial_value)
    column_state = [empty_state(slice_rows, feature_count) for local in range(local_blocks)]
    for offset in range(1, offset_count + 1):
        earlier = passed_along(my_slice, "own", offset)
        back_states = [empty_state(slice_rows, feature_count) for local in range(local_blocks)]
        for local in range(local_blocks):
            query_block = block_of(own_index, local)
            query_valid = full_rows < pick_entry(row_counts, query_block)
            for other in range(local_blocks):
                source = block_of(own_index - offset, other)
                scores = tile_scores(normed[local], earlier[other])
                row_top, row_total, partial_value = row_stats(
                    scores, key_mask(query_block, source), earlier[other]
                )
                running[local] = fold_in(running[local], row_top, row_total, partial_value)
                back_mask = (
                    linked_to(query_block, source) & query_valid[None, :] & (my_rows[:, None] >= 0)
                )
                back_top, back_total, back_sum = row_stats(scores.T, back_mask, normed[local])
                back_states[other] = fold_in(back_states[other], back_top, back_total, back_sum)
        stacked_back = stack_states(back_states)
        returned = passed_along((stacked_back[0], stacked_back[1], stacked_back[2]), "own", -offset)
        later_inside = own_index + offset < own_count
        for local in range(local_blocks):
            column_state[local] = fold_in(
                column_state[local],
                jnp.where(later_inside, returned[0][local], negative),
                jnp.where(later_inside, returned[1][local], 0.0),
                jnp.where(later_inside, returned[2][local], 0.0),
            )
    reduced = own_rows(stack_states(running), slice_rows, pair_count)
    result_state = combine_states(reduced, stack_states(column_state))
    run_max, run_mass, run_sum = result_state
    my_counts = jnp.stack(
        [pick_entry(row_counts, block_of(own_index, local)) for local in range(local_blocks)]
    )
    row_valid = my_rows[None, :] < my_counts[:, None]
    near_sums = jnp.where(row_valid[..., None], run_sum / run_mass[..., None], 0.0).astype(
        jnp.bfloat16
    )
    log_masses = jnp.where(row_valid, run_max + jnp.log(run_mass), 0.0)
    return (near_sums, log_masses)


MESH = pl.DeviceIdType.MESH


def kernel(
    groups, blocks, rows, slice_rows, block_total,
    sizes_hbm, counts_hbm, emb_hbm, near_ref, mass_ref,
    sizes_ref, counts_ref, emb_ref, queries, keys, top, mass, total,
    chip_out, chip_in, chip_stats_out, chip_stats_in,
    pair_out, pair_in, pair_stats_out, pair_stats_in,
    load, share_send, share_recv, direct_send, key_recv, relay_send,
    chip_send, chip_recv, pair_send, pair_recv,
):
    width = emb_ref.shape[2]
    mine = lax.axis_index("own")
    half = lax.axis_index("pair")
    group, core = mine // 2, mine % 2
    toward = 1 - 2 * (group % 2)
    across = group + toward
    ahead, behind = group + 2 * toward, group - 2 * toward
    has_ahead = (ahead >= 0) & (ahead < groups)
    has_behind = (behind >= 0) & (behind < groups)
    behind2 = group - 4 * toward
    has_behind2 = (behind2 >= 0) & (behind2 < groups)
    slots = 2 * blocks
    half_rows = rows // 2
    core_rows = blocks * rows
    slot_keys = slots * slice_rows

    def device(group_index, core_index):
        return (group_index * 2 + core_index, half)

    partner = (mine, 1 - half)
    sibling = device(group, 1 - core)

    def half_span(side):
        return pl.ds(pl.multiple_of(side * half_rows, half_rows), half_rows)

    def load_rows(index, side):
        return pltpu.make_async_copy(
            emb_hbm.at[:, half_span(side)], emb_ref.at[:, half_span(side)], load.at[index]
        )

    load_rows(0, half).start()
    load_rows(1, 1 - half).start()
    load_sizes = pltpu.make_async_copy(sizes_hbm, sizes_ref, load.at[2])
    load_counts = pltpu.make_async_copy(counts_hbm, counts_ref, load.at[3])
    load_sizes.start()
    load_counts.start()

    barrier = pltpu.get_barrier_semaphore()

    def greet(target):
        pl.semaphore_signal(barrier, inc=1, device_id=target, device_id_type=MESH)

    greet(sibling)
    greet(partner)
    for other_core in range(2):
        greet(device(across, other_core))

    @pl.when(has_ahead)
    def _():
        for other_core in range(2):
            greet(device(ahead, other_core))

    @pl.when(has_behind)
    def _():
        for other_core in range(2):
            greet(device(behind, other_core))

    def normalise(side):
        for local in range(blocks):
            values = emb_ref[local, half_span(side), :]
            squares = jnp.sum(values * values, axis=-1, keepdims=True)
            queries[core * blocks + local, half_span(side), :] = (
                values * lax.rsqrt(squares + 1e-06)
            ).astype(jnp.bfloat16)

    load_rows(0, half).wait()
    normalise(half)

    own_blocks = pl.ds(core * blocks, blocks)
    other_blocks = pl.ds((1 - core) * blocks, blocks)

    def key_rows(core_index):
        return pl.ds(pl.multiple_of((half * 2 + core_index) * slice_rows, slice_rows), slice_rows)

    def share(index, side):
        return pltpu.make_async_remote_copy(
            src_ref=queries.at[own_blocks, half_span(side)],
            dst_ref=queries.at[own_blocks, half_span(side)],
            send_sem=share_send.at[index],
            recv_sem=share_recv.at[index],
            device_id=sibling,
            device_id_type=MESH,
        )

    def share_in(index, side):
        return pltpu.make_async_remote_copy(
            src_ref=queries.at[other_blocks, half_span(side)],
            dst_ref=queries.at[other_blocks, half_span(side)],
            send_sem=share_send.at[index],
            recv_sem=share_recv.at[index],
            device_id=sibling,
            device_id_type=MESH,
        )

    def direct(place, target, slot, other_core, local):
        block = core * blocks + local
        return pltpu.make_async_remote_copy(
            src_ref=queries.at[block, key_rows(other_core)],
            dst_ref=keys.at[slot, block],
            send_sem=direct_send.at[place, other_core, local],
            recv_sem=key_recv.at[slot, block],
            device_id=device(target, other_core),
            device_id_type=MESH,
        )

    def relay(place, source, target, slot, block):
        return pltpu.make_async_remote_copy(
            src_ref=keys.at[source, block],
            dst_ref=keys.at[slot, block],
            send_sem=relay_send.at[place, block],
            recv_sem=key_recv.at[slot, block],
            device_id=device(target, core),
            device_id_type=MESH,
        )

    def arrived(slot, block):
        relay(0, slot, across, slot, block).wait_recv()

    def direct_across(other_core, local):
        return direct(0, across, 1, other_core, local)

    def direct_ahead(other_core, local):
        return direct(1, ahead, 3, other_core, local)

    def direct_behind(other_core, local):
        return direct(2, behind, 2, other_core, local)

    skip = (1 - toward) // 2
    reach = slots - 1

    def upper(index):
        return index + 1 - skip

    def lower(index):
        return index + skip

    def relay_across(index):
        return relay(0, 2, across, 4, (index + skip) % slots)

    def relay_behind(index):
        return relay(1, 1, behind, 5, lower(index))

    def relay_ahead(index):
        return relay(2, 4, ahead, 6, upper(index))

    neighbours = 4 + 2 * has_ahead.astype(jnp.int32) + 2 * has_behind.astype(jnp.int32)
    pl.semaphore_wait(barrier, neighbours)

    for other_core in range(2):
        for local in range(blocks):
            direct_across(other_core, local).start()

            @pl.when(has_behind)
            def _():
                direct_behind(other_core, local).start()

            @pl.when(has_ahead)
            def _():
                direct_ahead(other_core, local).start()

    share(0, half).start()
    load_rows(1, 1 - half).wait()
    normalise(1 - half)
    share(1, 1 - half).start()
    load_sizes.wait()
    load_counts.wait()

    starts = []
    so_far = jnp.int32(0)
    for cluster in range(sizes_ref.shape[0]):
        starts.append(so_far)
        so_far = so_far + sizes_ref[cluster]

    def cluster_of(ids):
        return sum((ids >= start).astype(jnp.int32) for start in starts)

    top[...] = jnp.full_like(top, negative)
    mass[...] = jnp.zeros_like(mass)
    total[...] = jnp.zeros_like(total)

    @pl.when(jnp.logical_not(has_ahead))
    def _():
        keys[2] = jnp.zeros_like(keys[2])
        keys[5] = jnp.zeros_like(keys[5])

    @pl.when(jnp.logical_not(has_behind))
    def _():
        keys[3] = jnp.zeros_like(keys[3])
        keys[4] = jnp.zeros_like(keys[4])

    @pl.when(has_ahead)
    def _():
        keys[5, lower(reach) % slots] = jnp.zeros_like(keys[5, 0])

    @pl.when(has_behind2)
    def _():
        keys[6, upper(reach) % slots] = jnp.zeros_like(keys[6, 0])

    @pl.when(jnp.logical_not(has_behind2))
    def _():
        keys[6] = jnp.zeros_like(keys[6])

    own_slot = 0

    def fold(first_slot, distances, side_core):
        taken = len(distances)
        lane_ids = lax.broadcasted_iota(jnp.int32, (1, taken * slot_keys), 1)
        lane_local = lane_ids % slot_keys
        lane_row = lane_local % slice_rows + (half * 2 + core) * slice_rows
        lane_block = jnp.zeros_like(lane_ids)
        valid = jnp.zeros_like(lane_ids)
        for index, distance in enumerate(distances):
            first_block = (group + toward * distance) * slots
            for local in range(slots):
                block = first_block + local
                there = lane_ids // slice_rows == index * slots + local
                inside = (block >= 0) & (block < block_total)
                count = counts_ref[jnp.clip(block, 0, block_total - 1)]
                valid = jnp.where(there, jnp.where(inside, count, 0), valid)
                lane_block = jnp.where(there, block, lane_block)
        key_cluster = jnp.where(lane_row < valid, cluster_of(lane_block), -1)
        row_ids = lax.broadcasted_iota(jnp.int32, (core_rows, 1), 0) + (
            (group * 2 + side_core) * core_rows
        )
        query_cluster = cluster_of(row_ids // rows)
        block_keys = keys[first_slot:first_slot + taken] if isinstance(first_slot, int) else (
            keys[pl.ds(first_slot, taken)]
        )
        block_keys = block_keys.reshape(taken * slot_keys, width)
        side_blocks = pl.ds(side_core * blocks, blocks)
        span = pl.ds(pl.multiple_of(side_core * core_rows, core_rows), core_rows)
        scores = sharpness * lax.dot_general(
            queries[side_blocks].reshape(core_rows, width), block_keys,
            (((1,), (1,)), ((), ())), preferred_element_type=jnp.float32,
        )
        kept = query_cluster == key_cluster
        if first_slot is own_slot:
            kept = kept & (row_ids != lane_block * rows + lane_row)
        scores = jnp.where(kept, scores, 2.0 * negative)
        old_top = top[span]
        new_top = jnp.maximum(old_top, jnp.max(scores, axis=1, keepdims=True))
        scale = jnp.exp(old_top - new_top)
        weight = jnp.exp(scores - new_top)
        top[span] = new_top
        mass[span] = mass[span] * scale + jnp.sum(weight, axis=1, keepdims=True)
        weight = weight.astype(jnp.bfloat16)
        piece = min(256, width)
        for column in range(0, width, piece):
            columns = slice(column, column + piece)
            total[span, columns] = total[span, columns] * scale + jnp.dot(
                weight, block_keys[:, columns], preferred_element_type=jnp.float32
            )

    share_in(0, half).wait_recv()
    keys[0] = queries[:, key_rows(core), :]
    share_in(1, 1 - half).wait_recv()

    def own_fold(side_core, carry):
        fold(own_slot, (0,), side_core)
        return carry

    lax.fori_loop(0, 2, own_fold, 0)

    early = slots // 2

    def pair_fold(turn, carry):
        @pl.when(turn == 0)
        def _():
            @pl.when(has_ahead)
            def _():
                for index in range(slots):
                    arrived(2, (index + skip) % slots)
                    if index < early:
                        relay_across(index).start()

            for index in range(reach):
                arrived(1, lower(index))

                @pl.when(has_behind)
                def _():
                    relay_behind(index).start()

            arrived(1, lower(reach) % slots)

        @pl.when((turn == 2) & has_ahead)
        def _():
            for index in range(early, slots):
                relay_across(index).start()

        @pl.when((turn == 2) & has_behind)
        def _():
            for index in range(reach):
                arrived(4, upper(index))

                @pl.when(has_ahead)
                def _():
                    relay_ahead(index).start()

            arrived(4, upper(reach) % slots)
            for block in range(slots):
                arrived(3, block)

        late = turn // 2
        fold(1 + 2 * late, (1 - 3 * late, 2 - 3 * late), turn % 2)
        return carry

    lax.fori_loop(0, 4, pair_fold, 0)

    eye = (
        lax.broadcasted_iota(jnp.int32, (half_rows, half_rows), 0)
        == lax.broadcasted_iota(jnp.int32, (half_rows, half_rows), 1)
    )

    def to_lanes(column):
        return jnp.sum(jnp.where(eye, column, 0.0), axis=0, keepdims=True)

    def to_rows(lanes):
        return jnp.sum(jnp.where(eye, lanes, 0.0), axis=1, keepdims=True)

    def rows_of(block, side):
        return pl.ds(pl.multiple_of(block * rows + side * half_rows, half_rows), half_rows)

    def sent(source, target, send, recv, index, destination):
        return pltpu.make_async_remote_copy(
            src_ref=source, dst_ref=target, send_sem=send.at[index], recv_sem=recv.at[index],
            device_id=destination, device_id_type=MESH,
        )

    def chip_copy(remote):
        return sent(chip_out.at[remote], chip_in.at[remote], chip_send, chip_recv, remote, sibling)

    def pair_copy(local):
        return sent(pair_out.at[local], pair_in.at[local], pair_send, pair_recv, local, partner)

    chip_stats = sent(chip_stats_out, chip_stats_in, chip_send, chip_recv, 2, sibling)
    pair_stats = sent(pair_stats_out, pair_stats_in, pair_send, pair_recv, blocks, partner)
    sides = (1 - half, half)

    @pl.when(has_ahead)
    def _():
        for index in range(reach):
            arrived(5, lower(index))

    def late_fold(side_core, carry):
        fold(5, (3,), side_core)
        return carry

    lax.fori_loop(0, 2, late_fold, 0)

    @pl.when(has_behind2)
    def _():
        for index in range(reach):
            arrived(6, upper(index))

    def last_fold(turn, carry):
        fold(6, (-3,), jnp.where(turn == 0, 1 - core, core))

        @pl.when(turn == 0)
        def _():
            for remote in range(2):
                for local in range(blocks):
                    span = rows_of((1 - core) * blocks + local, sides[remote])
                    place = remote * blocks + local
                    chip_stats_out[place, 0:1, :half_rows] = to_lanes(top[span])
                    chip_stats_out[place, 1:2, :half_rows] = to_lanes(mass[span])
            chip_stats.start()
            for remote in range(2):
                for local in range(blocks):
                    span = rows_of((1 - core) * blocks + local, sides[remote])
                    chip_out[remote, local] = total[span].astype(jnp.bfloat16)
                chip_copy(remote).start()

        return carry

    lax.fori_loop(0, 2, last_fold, 0)

    chip_stats.wait_recv()
    scales = {}
    for remote in range(2):
        for local in range(blocks):
            span = rows_of(core * blocks + local, sides[remote])
            place = remote * blocks + local
            other_top = to_rows(chip_stats_in[place, 0:1, :half_rows])
            other_mass = to_rows(chip_stats_in[place, 1:2, :half_rows])
            new_top = jnp.maximum(top[span], other_top)
            scale = jnp.exp(top[span] - new_top)
            other_scale = jnp.exp(other_top - new_top)
            new_mass = mass[span] * scale + other_mass * other_scale
            scales[remote, local] = (scale, other_scale, new_top, new_mass)
            if remote == 0:
                pair_stats_out[local, 0:1, :half_rows] = to_lanes(new_top)
                pair_stats_out[local, 1:2, :half_rows] = to_lanes(new_mass)
    pair_stats.start()
    for remote in range(2):
        chip_copy(remote).wait_recv()
        for local in range(blocks):
            span = rows_of(core * blocks + local, sides[remote])
            scale, other_scale, new_top, new_mass = scales[remote, local]
            new_total = total[span] * scale + chip_in[remote, local].astype(jnp.float32) * other_scale
            if remote == 0:
                pair_out[local] = new_total.astype(jnp.bfloat16)
                pair_copy(local).start()
            else:
                total[span] = new_total

    place = lax.broadcasted_iota(jnp.int32, (half_rows, 1), 0) + half * half_rows
    pair_stats.wait_recv()
    final = []
    for local in range(blocks):
        other_top = to_rows(pair_stats_in[local, 0:1, :half_rows])
        other_mass = to_rows(pair_stats_in[local, 1:2, :half_rows])
        _, _, own_top, own_mass = scales[1, local]
        new_top = jnp.maximum(own_top, other_top)
        scale = jnp.exp(own_top - new_top)
        other_scale = jnp.exp(other_top - new_top)
        new_mass = own_mass * scale + other_mass * other_scale
        row_valid = place < counts_ref[mine * blocks + local]
        final.append((scale / new_mass, other_scale / new_mass, row_valid))
        logs = jnp.where(row_valid, new_top + jnp.log(new_mass), 0.0)
        mass_ref[local:local + 1, :] = to_lanes(logs)

    share(0, half).wait_send()
    share(1, 1 - half).wait_send()
    for other_core in range(2):
        for local in range(blocks):
            direct_across(other_core, local).wait_send()

            @pl.when(has_ahead)
            def _():
                direct_ahead(other_core, local).wait_send()

            @pl.when(has_behind)
            def _():
                direct_behind(other_core, local).wait_send()

    @pl.when(has_ahead)
    def _():
        for index in range(slots):
            relay_across(index).wait_send()

    @pl.when(has_behind)
    def _():
        for index in range(reach):
            relay_behind(index).wait_send()

    @pl.when(has_ahead & has_behind)
    def _():
        for index in range(reach):
            relay_ahead(index).wait_send()

    chip_stats.wait_send()
    pair_stats.wait_send()
    for remote in range(2):
        chip_copy(remote).wait_send()

    for local in range(blocks):
        pair_copy(local).wait_recv()
        span = rows_of(core * blocks + local, half)
        scale, other_scale, row_valid = final[local]
        merged = total[span] * scale + pair_in[local].astype(jnp.float32) * other_scale
        near_ref[local] = jnp.where(row_valid, merged, 0.0).astype(jnp.bfloat16)

    for local in range(blocks):
        pair_copy(local).wait_send()


def kernel_body(embeddings, cluster_sizes, row_counts):
    blocks, rows, width = embeddings.shape
    groups = lax.axis_size("own") // 2
    slots, slice_rows, half_rows = 2 * blocks, rows // 4, rows // 2
    query_rows = slots * rows
    wide, narrow = jnp.float32, jnp.bfloat16
    stats = (8, 128)
    dma = pltpu.SemaphoreType.DMA
    hbm, vmem = pl.BlockSpec(memory_space=pltpu.HBM), pl.BlockSpec(memory_space=pltpu.VMEM)
    return pl.pallas_call(
        functools.partial(kernel, groups, blocks, rows, slice_rows, row_counts.shape[0]),
        out_shape=(
            jax.ShapeDtypeStruct((blocks, half_rows, width), narrow),
            jax.ShapeDtypeStruct((blocks, half_rows), wide),
        ),
        in_specs=[hbm, hbm, hbm],
        out_specs=(vmem, vmem),
        scratch_shapes=[
            pltpu.SMEM(cluster_sizes.shape, jnp.int32),
            pltpu.SMEM(row_counts.shape, jnp.int32),
            pltpu.VMEM(embeddings.shape, wide),
            pltpu.VMEM((slots, rows, width), narrow),
            pltpu.VMEM((7, slots, slice_rows, width), narrow),
            pltpu.VMEM((query_rows, 1), wide),
            pltpu.VMEM((query_rows, 1), wide),
            pltpu.VMEM((query_rows, width), wide),
            pltpu.VMEM((2, blocks, half_rows, width), narrow),
            pltpu.VMEM((2, blocks, half_rows, width), narrow),
            pltpu.VMEM((2 * blocks, *stats), wide),
            pltpu.VMEM((2 * blocks, *stats), wide),
            pltpu.VMEM((blocks, half_rows, width), narrow),
            pltpu.VMEM((blocks, half_rows, width), narrow),
            pltpu.VMEM((blocks, *stats), wide),
            pltpu.VMEM((blocks, *stats), wide),
            dma((4,)), dma((2,)), dma((2,)),
            dma((3, 2, blocks)), dma((7, slots)), dma((3, slots)),
            dma((3,)), dma((3,)), dma((blocks + 1,)), dma((blocks + 1,)),
        ],
        compiler_params=pltpu.CompilerParams(
            collective_id=0, has_side_effects=True, vmem_limit_bytes=56 * 1024 * 1024
        ),
        cost_estimate=pl.CostEstimate(
            flops=4 * query_rows * 7 * slots * slice_rows * width,
            bytes_accessed=embeddings.size * 4,
            transcendentals=query_rows * 7 * slots * slice_rows,
        ),
    )(cluster_sizes, row_counts, embeddings)


def fits_kernel(block_shape):
    blocks, rows, width = block_shape
    covered = (SPAN + 2 * blocks - 2) // (2 * blocks) <= 3
    far_enough = 3 * 2 * blocks >= SPAN
    whole_tiles = rows % 128 == 0 and width % 128 == 0
    return lax.axis_size("pair") == 2 and lax.axis_size("own") % 4 == 0 and (
        covered and far_enough and whole_tiles
    )


def device_part(embeddings, cluster_sizes, row_counts):
    chosen = kernel_body if fits_kernel(embeddings.shape) else body
    return chosen(embeddings, cluster_sizes, row_counts)


def solution(mesh):
    placed = (P("own", None, None), P(), P())
    return jax.shard_map(
        device_part,
        mesh=mesh,
        in_specs=placed,
        out_specs=(P("own", "pair", None), P("own", "pair")),
        check_vma=False,
    )
```

```python
import functools

import jax
import jax.numpy as jnp
from jax import lax
from jax.experimental import pallas as pl
from jax.experimental.pallas import tpu as pltpu
from jax.sharding import PartitionSpec as P

SPAN = 12


sharpness = 128.0
negative = -1e30


def passed_along(shard, axis, by):
    count = lax.axis_size(axis)
    pairs = [(i, i + by) for i in range(count) if 0 <= i + by < count]
    return lax.ppermute(shard, axis, pairs)


def unit_rows(values):
    squares = jnp.sum(values * values, axis=-1, keepdims=True)
    return (values * lax.rsqrt(squares + 1e-06)).astype(jnp.bfloat16)


def fold_in(running, row_top, row_total, partial_value):
    run_max, run_mass, run_sum = running
    new_max = jnp.maximum(run_max, row_top)
    old_scale = jnp.exp(run_max - new_max)
    new_scale = jnp.exp(row_top - new_max)
    return (
        new_max,
        run_mass * old_scale + row_total * new_scale,
        run_sum * old_scale[..., None] + partial_value * new_scale[..., None],
    )


def combine_states(first_state, second_state):
    return fold_in(first_state, second_state[0], second_state[1], second_state[2])


def row_stats(scores, kept, key_rows):
    scores = jnp.where(kept, scores, negative)
    row_top = jnp.max(scores, axis=1)
    weight = jnp.where(kept, jnp.exp(scores - row_top[:, None]), 0.0)
    partial_value = jnp.dot(
        weight.astype(jnp.bfloat16), key_rows, preferred_element_type=jnp.float32
    )
    return (row_top, jnp.sum(weight, axis=1), partial_value)


def pick_entry(table, position):
    places = jnp.arange(table.shape[0], dtype=jnp.int32)
    return jnp.sum(jnp.where(places == position, table, 0))


def empty_state(row_total, feature_count):
    return (
        jnp.full((row_total,), negative, jnp.float32),
        jnp.zeros((row_total,), jnp.float32),
        jnp.zeros((row_total, feature_count), jnp.float32),
    )


def stack_states(states):
    return tuple((jnp.stack([state[field] for state in states]) for field in range(3)))


def own_rows(stacked, slice_rows, pair_count):
    run_max, run_mass, run_sum = stacked
    local_blocks = run_max.shape[0]
    feature_count = run_sum.shape[2]
    arrived = (
        lax.all_to_all(
            run_max.reshape(local_blocks, pair_count, slice_rows),
            "pair",
            split_axis=1,
            concat_axis=1,
            tiled=True,
        ),
        lax.all_to_all(
            run_mass.reshape(local_blocks, pair_count, slice_rows),
            "pair",
            split_axis=1,
            concat_axis=1,
            tiled=True,
        ),
        lax.all_to_all(
            run_sum.reshape(local_blocks, pair_count, slice_rows, feature_count),
            "pair",
            split_axis=1,
            concat_axis=1,
            tiled=True,
        ),
    )
    new_max = jnp.max(arrived[0], axis=1)
    scales = jnp.exp(arrived[0] - new_max[:, None, :])
    return (
        new_max,
        jnp.sum(arrived[1] * scales, axis=1),
        jnp.sum(arrived[2] * scales[..., None], axis=1),
    )


def body(embeddings, cluster_sizes, row_counts):
    normed = unit_rows(embeddings)
    local_blocks, block_rows, feature_count = normed.shape
    pair_count = lax.axis_size("pair")
    own_count = lax.axis_size("own")
    block_total = own_count * local_blocks
    slice_rows = block_rows // pair_count
    own_index = lax.axis_index("own")
    slice_start = lax.axis_index("pair") * slice_rows
    my_slice = lax.dynamic_slice_in_dim(normed, slice_start, slice_rows, 1)
    cluster_start = jnp.cumsum(cluster_sizes) - cluster_sizes
    block_ids = jnp.arange(block_total, dtype=jnp.int32)
    owner_cluster = (
        jnp.sum((block_ids[:, None] >= cluster_start[None, :]).astype(jnp.int32), axis=1) - 1
    )
    full_rows = jnp.arange(block_rows, dtype=jnp.int32)
    my_rows = slice_start + jnp.arange(slice_rows, dtype=jnp.int32)
    offset_count = (SPAN + local_blocks - 2) // local_blocks

    def block_of(owner, local):
        return owner * local_blocks + local

    def linked_to(query_block, source):
        inside = (source >= 0) & (source < block_total)
        return inside & (
            pick_entry(owner_cluster, source) == pick_entry(owner_cluster, query_block)
        )

    def key_mask(query_block, source):
        valid_keys = my_rows[None, :] < pick_entry(row_counts, source)
        not_self = (query_block != source) | (full_rows[:, None] != my_rows[None, :])
        return linked_to(query_block, source) & valid_keys & not_self

    def tile_scores(queries, key_rows):
        return sharpness * jnp.dot(queries, key_rows.T, preferred_element_type=jnp.float32)

    running = [empty_state(block_rows, feature_count) for local in range(local_blocks)]
    for local in range(local_blocks):
        query_block = block_of(own_index, local)
        for other in range(local_blocks):
            source = block_of(own_index, other)
            row_top, row_total, partial_value = row_stats(
                tile_scores(normed[local], my_slice[other]),
                key_mask(query_block, source),
                my_slice[other],
            )
            running[local] = fold_in(running[local], row_top, row_total, partial_value)
    column_state = [empty_state(slice_rows, feature_count) for local in range(local_blocks)]
    for offset in range(1, offset_count + 1):
        earlier = passed_along(my_slice, "own", offset)
        back_states = [empty_state(slice_rows, feature_count) for local in range(local_blocks)]
        for local in range(local_blocks):
            query_block = block_of(own_index, local)
            query_valid = full_rows < pick_entry(row_counts, query_block)
            for other in range(local_blocks):
                source = block_of(own_index - offset, other)
                scores = tile_scores(normed[local], earlier[other])
                row_top, row_total, partial_value = row_stats(
                    scores, key_mask(query_block, source), earlier[other]
                )
                running[local] = fold_in(running[local], row_top, row_total, partial_value)
                back_mask = (
                    linked_to(query_block, source) & query_valid[None, :] & (my_rows[:, None] >= 0)
                )
                back_top, back_total, back_sum = row_stats(scores.T, back_mask, normed[local])
                back_states[other] = fold_in(back_states[other], back_top, back_total, back_sum)
        stacked_back = stack_states(back_states)
        returned = passed_along((stacked_back[0], stacked_back[1], stacked_back[2]), "own", -offset)
        later_inside = own_index + offset < own_count
        for local in range(local_blocks):
            column_state[local] = fold_in(
                column_state[local],
                jnp.where(later_inside, returned[0][local], negative),
                jnp.where(later_inside, returned[1][local], 0.0),
                jnp.where(later_inside, returned[2][local], 0.0),
            )
    reduced = own_rows(stack_states(running), slice_rows, pair_count)
    result_state = combine_states(reduced, stack_states(column_state))
    run_max, run_mass, run_sum = result_state
    my_counts = jnp.stack(
        [pick_entry(row_counts, block_of(own_index, local)) for local in range(local_blocks)]
    )
    row_valid = my_rows[None, :] < my_counts[:, None]
    near_sums = jnp.where(row_valid[..., None], run_sum / run_mass[..., None], 0.0).astype(
        jnp.bfloat16
    )
    log_masses = jnp.where(row_valid, run_max + jnp.log(run_mass), 0.0)
    return (near_sums, log_masses)


MESH = pl.DeviceIdType.MESH


def kernel(
    groups, blocks, rows, slice_rows, block_total,
    sizes_hbm, counts_hbm, emb_hbm, near_ref, mass_ref,
    sizes_ref, counts_ref, emb_ref, queries, keys, top, mass, total,
    chip_out, chip_in, chip_stats_out, chip_stats_in,
    pair_out, pair_in, pair_stats_out, pair_stats_in,
    load, share_send, share_recv, direct_send, key_recv, relay_send,
    chip_send, chip_recv, pair_send, pair_recv,
):
    width = emb_ref.shape[2]
    mine = lax.axis_index("own")
    half = lax.axis_index("pair")
    group, core = mine // 2, mine % 2
    toward = 1 - 2 * (group % 2)
    across = group + toward
    ahead, behind = group + 2 * toward, group - 2 * toward
    has_ahead = (ahead >= 0) & (ahead < groups)
    has_behind = (behind >= 0) & (behind < groups)
    behind2 = group - 4 * toward
    has_behind2 = (behind2 >= 0) & (behind2 < groups)
    slots = 2 * blocks
    half_rows = rows // 2
    core_rows = blocks * rows
    slot_keys = slots * slice_rows

    def device(group_index, core_index):
        return (group_index * 2 + core_index, half)

    partner = (mine, 1 - half)
    sibling = device(group, 1 - core)

    def half_span(side):
        return pl.ds(pl.multiple_of(side * half_rows, half_rows), half_rows)

    def load_rows(index, side):
        return pltpu.make_async_copy(
            emb_hbm.at[:, half_span(side)], emb_ref.at[:, half_span(side)], load.at[index]
        )

    load_rows(0, half).start()
    load_rows(1, 1 - half).start()
    load_sizes = pltpu.make_async_copy(sizes_hbm, sizes_ref, load.at[2])
    load_counts = pltpu.make_async_copy(counts_hbm, counts_ref, load.at[3])
    load_sizes.start()
    load_counts.start()

    barrier = pltpu.get_barrier_semaphore()

    def greet(target):
        pl.semaphore_signal(barrier, inc=1, device_id=target, device_id_type=MESH)

    greet(sibling)
    greet(partner)
    for other_core in range(2):
        greet(device(across, other_core))

    @pl.when(has_ahead)
    def _():
        for other_core in range(2):
            greet(device(ahead, other_core))

    @pl.when(has_behind)
    def _():
        for other_core in range(2):
            greet(device(behind, other_core))

    def normalise(side):
        for local in range(blocks):
            values = emb_ref[local, half_span(side), :]
            squares = jnp.sum(values * values, axis=-1, keepdims=True)
            queries[core * blocks + local, half_span(side), :] = (
                values * lax.rsqrt(squares + 1e-06)
            ).astype(jnp.bfloat16)

    load_rows(0, half).wait()
    normalise(half)

    own_blocks = pl.ds(core * blocks, blocks)
    other_blocks = pl.ds((1 - core) * blocks, blocks)

    def key_rows(core_index):
        return pl.ds(pl.multiple_of((half * 2 + core_index) * slice_rows, slice_rows), slice_rows)

    def share(index, side):
        return pltpu.make_async_remote_copy(
            src_ref=queries.at[own_blocks, half_span(side)],
            dst_ref=queries.at[own_blocks, half_span(side)],
            send_sem=share_send.at[index],
            recv_sem=share_recv.at[index],
            device_id=sibling,
            device_id_type=MESH,
        )

    def share_in(index, side):
        return pltpu.make_async_remote_copy(
            src_ref=queries.at[other_blocks, half_span(side)],
            dst_ref=queries.at[other_blocks, half_span(side)],
            send_sem=share_send.at[index],
            recv_sem=share_recv.at[index],
            device_id=sibling,
            device_id_type=MESH,
        )

    def direct(place, target, slot, other_core, local):
        block = core * blocks + local
        return pltpu.make_async_remote_copy(
            src_ref=queries.at[block, key_rows(other_core)],
            dst_ref=keys.at[slot, block],
            send_sem=direct_send.at[place, other_core, local],
            recv_sem=key_recv.at[slot, block],
            device_id=device(target, other_core),
            device_id_type=MESH,
        )

    def relay(place, source, target, slot, block):
        return pltpu.make_async_remote_copy(
            src_ref=keys.at[source, block],
            dst_ref=keys.at[slot, block],
            send_sem=relay_send.at[place, block],
            recv_sem=key_recv.at[slot, block],
            device_id=device(target, core),
            device_id_type=MESH,
        )

    def arrived(slot, block):
        relay(0, slot, across, slot, block).wait_recv()

    def direct_across(other_core, local):
        return direct(0, across, 1, other_core, local)

    def direct_ahead(other_core, local):
        return direct(1, ahead, 3, other_core, local)

    def direct_behind(other_core, local):
        return direct(2, behind, 2, other_core, local)

    skip = (1 - toward) // 2
    reach = slots - 1

    def upper(index):
        return index + 1 - skip

    def lower(index):
        return index + skip

    def relay_across(index):
        return relay(0, 2, across, 4, (index + skip) % slots)

    def relay_behind(index):
        return relay(1, 1, behind, 5, lower(index))

    def relay_ahead(index):
        return relay(2, 4, ahead, 6, upper(index))

    neighbours = 4 + 2 * has_ahead.astype(jnp.int32) + 2 * has_behind.astype(jnp.int32)
    pl.semaphore_wait(barrier, neighbours)

    for other_core in range(2):
        for local in range(blocks):
            direct_across(other_core, local).start()

            @pl.when(has_behind)
            def _():
                direct_behind(other_core, local).start()

            @pl.when(has_ahead)
            def _():
                direct_ahead(other_core, local).start()

    share(0, half).start()
    load_rows(1, 1 - half).wait()
    normalise(1 - half)
    share(1, 1 - half).start()
    load_sizes.wait()
    load_counts.wait()

    starts = []
    so_far = jnp.int32(0)
    for cluster in range(sizes_ref.shape[0]):
        starts.append(so_far)
        so_far = so_far + sizes_ref[cluster]

    def cluster_of(ids):
        return sum((ids >= start).astype(jnp.int32) for start in starts)

    top[...] = jnp.full_like(top, negative)
    mass[...] = jnp.zeros_like(mass)
    total[...] = jnp.zeros_like(total)

    @pl.when(jnp.logical_not(has_ahead))
    def _():
        keys[2] = jnp.zeros_like(keys[2])
        keys[5] = jnp.zeros_like(keys[5])

    @pl.when(jnp.logical_not(has_behind))
    def _():
        keys[3] = jnp.zeros_like(keys[3])
        keys[4] = jnp.zeros_like(keys[4])

    @pl.when(has_ahead)
    def _():
        keys[5, lower(reach) % slots] = jnp.zeros_like(keys[5, 0])

    @pl.when(has_behind2)
    def _():
        keys[6, upper(reach) % slots] = jnp.zeros_like(keys[6, 0])

    @pl.when(jnp.logical_not(has_behind2))
    def _():
        keys[6] = jnp.zeros_like(keys[6])

    own_slot = 0

    def fold(first_slot, distances, side_core):
        taken = len(distances)
        lane_ids = lax.broadcasted_iota(jnp.int32, (1, taken * slot_keys), 1)
        lane_local = lane_ids % slot_keys
        lane_row = lane_local % slice_rows + (half * 2 + core) * slice_rows
        lane_block = jnp.zeros_like(lane_ids)
        valid = jnp.zeros_like(lane_ids)
        for index, distance in enumerate(distances):
            first_block = (group + toward * distance) * slots
            for local in range(slots):
                block = first_block + local
                there = lane_ids // slice_rows == index * slots + local
                inside = (block >= 0) & (block < block_total)
                count = counts_ref[jnp.clip(block, 0, block_total - 1)]
                valid = jnp.where(there, jnp.where(inside, count, 0), valid)
                lane_block = jnp.where(there, block, lane_block)
        key_cluster = jnp.where(lane_row < valid, cluster_of(lane_block), -1)
        row_ids = lax.broadcasted_iota(jnp.int32, (core_rows, 1), 0) + (
            (group * 2 + side_core) * core_rows
        )
        query_cluster = cluster_of(row_ids // rows)
        block_keys = keys[first_slot:first_slot + taken] if isinstance(first_slot, int) else (
            keys[pl.ds(first_slot, taken)]
        )
        block_keys = block_keys.reshape(taken * slot_keys, width)
        side_blocks = pl.ds(side_core * blocks, blocks)
        span = pl.ds(pl.multiple_of(side_core * core_rows, core_rows), core_rows)
        scores = sharpness * lax.dot_general(
            queries[side_blocks].reshape(core_rows, width), block_keys,
            (((1,), (1,)), ((), ())), preferred_element_type=jnp.float32,
        )
        kept = query_cluster == key_cluster
        if first_slot is own_slot:
            kept = kept & (row_ids != lane_block * rows + lane_row)
        scores = jnp.where(kept, scores, 2.0 * negative)
        old_top = top[span]
        new_top = jnp.maximum(old_top, jnp.max(scores, axis=1, keepdims=True))
        scale = jnp.exp(old_top - new_top)
        weight = jnp.exp(scores - new_top)
        top[span] = new_top
        mass[span] = mass[span] * scale + jnp.sum(weight, axis=1, keepdims=True)
        weight = weight.astype(jnp.bfloat16)
        piece = min(256, width)
        for column in range(0, width, piece):
            columns = slice(column, column + piece)
            total[span, columns] = total[span, columns] * scale + jnp.dot(
                weight, block_keys[:, columns], preferred_element_type=jnp.float32
            )

    early = slots // 2

    @pl.when(has_ahead)
    def _():
        for index in range(slots):
            arrived(2, (index + skip) % slots)
            if index < early:
                relay_across(index).start()

    for index in range(reach):
        arrived(1, lower(index))

        @pl.when(has_behind)
        def _():
            relay_behind(index).start()

    arrived(1, lower(reach) % slots)

    share_in(0, half).wait_recv()
    keys[0] = queries[:, key_rows(core), :]
    share_in(1, 1 - half).wait_recv()

    def own_fold(side_core, carry):
        fold(own_slot, (0,), side_core)
        return carry

    lax.fori_loop(0, 2, own_fold, 0)

    def pair_fold(turn, carry):
        @pl.when((turn == 0) & has_ahead)
        def _():
            for index in range(early, slots):
                relay_across(index).start()

        @pl.when((turn == 2) & has_behind)
        def _():
            for index in range(reach):
                arrived(4, upper(index))

                @pl.when(has_ahead)
                def _():
                    relay_ahead(index).start()

            arrived(4, upper(reach) % slots)
            for block in range(slots):
                arrived(3, block)

        late = turn // 2
        fold(1 + 2 * late, (1 - 3 * late, 2 - 3 * late), turn % 2)
        return carry

    lax.fori_loop(0, 4, pair_fold, 0)

    eye = (
        lax.broadcasted_iota(jnp.int32, (half_rows, half_rows), 0)
        == lax.broadcasted_iota(jnp.int32, (half_rows, half_rows), 1)
    )

    def to_lanes(column):
        return jnp.sum(jnp.where(eye, column, 0.0), axis=0, keepdims=True)

    def to_rows(lanes):
        return jnp.sum(jnp.where(eye, lanes, 0.0), axis=1, keepdims=True)

    def rows_of(block, side):
        return pl.ds(pl.multiple_of(block * rows + side * half_rows, half_rows), half_rows)

    def sent(source, target, send, recv, index, destination):
        return pltpu.make_async_remote_copy(
            src_ref=source, dst_ref=target, send_sem=send.at[index], recv_sem=recv.at[index],
            device_id=destination, device_id_type=MESH,
        )

    def chip_copy(remote):
        return sent(chip_out.at[remote], chip_in.at[remote], chip_send, chip_recv, remote, sibling)

    def pair_copy(local):
        return sent(pair_out.at[local], pair_in.at[local], pair_send, pair_recv, local, partner)

    chip_stats = sent(chip_stats_out, chip_stats_in, chip_send, chip_recv, 2, sibling)
    pair_stats = sent(pair_stats_out, pair_stats_in, pair_send, pair_recv, blocks, partner)
    sides = (1 - half, half)

    @pl.when(has_ahead)
    def _():
        for index in range(reach):
            arrived(5, lower(index))

    def late_fold(side_core, carry):
        fold(5, (3,), side_core)
        return carry

    lax.fori_loop(0, 2, late_fold, 0)

    @pl.when(has_behind2)
    def _():
        for index in range(reach):
            arrived(6, upper(index))

    def last_fold(turn, carry):
        fold(6, (-3,), jnp.where(turn == 0, 1 - core, core))

        @pl.when(turn == 0)
        def _():
            for remote in range(2):
                for local in range(blocks):
                    span = rows_of((1 - core) * blocks + local, sides[remote])
                    place = remote * blocks + local
                    chip_stats_out[place, 0:1, :half_rows] = to_lanes(top[span])
                    chip_stats_out[place, 1:2, :half_rows] = to_lanes(mass[span])
            chip_stats.start()
            for remote in range(2):
                for local in range(blocks):
                    span = rows_of((1 - core) * blocks + local, sides[remote])
                    chip_out[remote, local] = total[span].astype(jnp.bfloat16)
                chip_copy(remote).start()

        return carry

    lax.fori_loop(0, 2, last_fold, 0)

    chip_stats.wait_recv()
    scales = {}
    for remote in range(2):
        for local in range(blocks):
            span = rows_of(core * blocks + local, sides[remote])
            place = remote * blocks + local
            other_top = to_rows(chip_stats_in[place, 0:1, :half_rows])
            other_mass = to_rows(chip_stats_in[place, 1:2, :half_rows])
            new_top = jnp.maximum(top[span], other_top)
            scale = jnp.exp(top[span] - new_top)
            other_scale = jnp.exp(other_top - new_top)
            new_mass = mass[span] * scale + other_mass * other_scale
            scales[remote, local] = (scale, other_scale, new_top, new_mass)
            if remote == 0:
                pair_stats_out[local, 0:1, :half_rows] = to_lanes(new_top)
                pair_stats_out[local, 1:2, :half_rows] = to_lanes(new_mass)
    pair_stats.start()
    for remote in range(2):
        chip_copy(remote).wait_recv()
        for local in range(blocks):
            span = rows_of(core * blocks + local, sides[remote])
            scale, other_scale, new_top, new_mass = scales[remote, local]
            new_total = total[span] * scale + chip_in[remote, local].astype(jnp.float32) * other_scale
            if remote == 0:
                pair_out[local] = new_total.astype(jnp.bfloat16)
                pair_copy(local).start()
            else:
                total[span] = new_total

    place = lax.broadcasted_iota(jnp.int32, (half_rows, 1), 0) + half * half_rows
    pair_stats.wait_recv()
    final = []
    for local in range(blocks):
        other_top = to_rows(pair_stats_in[local, 0:1, :half_rows])
        other_mass = to_rows(pair_stats_in[local, 1:2, :half_rows])
        _, _, own_top, own_mass = scales[1, local]
        new_top = jnp.maximum(own_top, other_top)
        scale = jnp.exp(own_top - new_top)
        other_scale = jnp.exp(other_top - new_top)
        new_mass = own_mass * scale + other_mass * other_scale
        row_valid = place < counts_ref[mine * blocks + local]
        final.append((scale / new_mass, other_scale / new_mass, row_valid))
        logs = jnp.where(row_valid, new_top + jnp.log(new_mass), 0.0)
        mass_ref[local:local + 1, :] = to_lanes(logs)

    share(0, half).wait_send()
    share(1, 1 - half).wait_send()
    for other_core in range(2):
        for local in range(blocks):
            direct_across(other_core, local).wait_send()

            @pl.when(has_ahead)
            def _():
                direct_ahead(other_core, local).wait_send()

            @pl.when(has_behind)
            def _():
                direct_behind(other_core, local).wait_send()

    @pl.when(has_ahead)
    def _():
        for index in range(slots):
            relay_across(index).wait_send()

    @pl.when(has_behind)
    def _():
        for index in range(reach):
            relay_behind(index).wait_send()

    @pl.when(has_ahead & has_behind)
    def _():
        for index in range(reach):
            relay_ahead(index).wait_send()

    chip_stats.wait_send()
    pair_stats.wait_send()
    for remote in range(2):
        chip_copy(remote).wait_send()

    for local in range(blocks):
        pair_copy(local).wait_recv()
        span = rows_of(core * blocks + local, half)
        scale, other_scale, row_valid = final[local]
        merged = total[span] * scale + pair_in[local].astype(jnp.float32) * other_scale
        near_ref[local] = jnp.where(row_valid, merged, 0.0).astype(jnp.bfloat16)

    for local in range(blocks):
        pair_copy(local).wait_send()


def kernel_body(embeddings, cluster_sizes, row_counts):
    blocks, rows, width = embeddings.shape
    groups = lax.axis_size("own") // 2
    slots, slice_rows, half_rows = 2 * blocks, rows // 4, rows // 2
    query_rows = slots * rows
    wide, narrow = jnp.float32, jnp.bfloat16
    stats = (8, 128)
    dma = pltpu.SemaphoreType.DMA
    hbm, vmem = pl.BlockSpec(memory_space=pltpu.HBM), pl.BlockSpec(memory_space=pltpu.VMEM)
    return pl.pallas_call(
        functools.partial(kernel, groups, blocks, rows, slice_rows, row_counts.shape[0]),
        out_shape=(
            jax.ShapeDtypeStruct((blocks, half_rows, width), narrow),
            jax.ShapeDtypeStruct((blocks, half_rows), wide),
        ),
        in_specs=[hbm, hbm, hbm],
        out_specs=(vmem, vmem),
        scratch_shapes=[
            pltpu.SMEM(cluster_sizes.shape, jnp.int32),
            pltpu.SMEM(row_counts.shape, jnp.int32),
            pltpu.VMEM(embeddings.shape, wide),
            pltpu.VMEM((slots, rows, width), narrow),
            pltpu.VMEM((7, slots, slice_rows, width), narrow),
            pltpu.VMEM((query_rows, 1), wide),
            pltpu.VMEM((query_rows, 1), wide),
            pltpu.VMEM((query_rows, width), wide),
            pltpu.VMEM((2, blocks, half_rows, width), narrow),
            pltpu.VMEM((2, blocks, half_rows, width), narrow),
            pltpu.VMEM((2 * blocks, *stats), wide),
            pltpu.VMEM((2 * blocks, *stats), wide),
            pltpu.VMEM((blocks, half_rows, width), narrow),
            pltpu.VMEM((blocks, half_rows, width), narrow),
            pltpu.VMEM((blocks, *stats), wide),
            pltpu.VMEM((blocks, *stats), wide),
            dma((4,)), dma((2,)), dma((2,)),
            dma((3, 2, blocks)), dma((7, slots)), dma((3, slots)),
            dma((3,)), dma((3,)), dma((blocks + 1,)), dma((blocks + 1,)),
        ],
        compiler_params=pltpu.CompilerParams(
            collective_id=0, has_side_effects=True, vmem_limit_bytes=56 * 1024 * 1024
        ),
        cost_estimate=pl.CostEstimate(
            flops=4 * query_rows * 7 * slots * slice_rows * width,
            bytes_accessed=embeddings.size * 4,
            transcendentals=query_rows * 7 * slots * slice_rows,
        ),
    )(cluster_sizes, row_counts, embeddings)


def fits_kernel(block_shape):
    blocks, rows, width = block_shape
    covered = (SPAN + 2 * blocks - 2) // (2 * blocks) <= 3
    far_enough = 3 * 2 * blocks >= SPAN
    whole_tiles = rows % 128 == 0 and width % 128 == 0
    return lax.axis_size("pair") == 2 and lax.axis_size("own") % 4 == 0 and (
        covered and far_enough and whole_tiles
    )


def device_part(embeddings, cluster_sizes, row_counts):
    chosen = kernel_body if fits_kernel(embeddings.shape) else body
    return chosen(embeddings, cluster_sizes, row_counts)


def solution(mesh):
    placed = (P("own", None, None), P(), P())
    return jax.shard_map(
        device_part,
        mesh=mesh,
        in_specs=placed,
        out_specs=(P("own", "pair", None), P("own", "pair")),
        check_vma=False,
    )
```

```python
import functools

import jax
import jax.numpy as jnp
from jax import lax
from jax.experimental import pallas as pl
from jax.experimental.pallas import tpu as pltpu
from jax.sharding import PartitionSpec as P

SPAN = 12


sharpness = 128.0
negative = -1e30


def passed_along(shard, axis, by):
    count = lax.axis_size(axis)
    pairs = [(i, i + by) for i in range(count) if 0 <= i + by < count]
    return lax.ppermute(shard, axis, pairs)


def unit_rows(values):
    squares = jnp.sum(values * values, axis=-1, keepdims=True)
    return (values * lax.rsqrt(squares + 1e-06)).astype(jnp.bfloat16)


def fold_in(running, row_top, row_total, partial_value):
    run_max, run_mass, run_sum = running
    new_max = jnp.maximum(run_max, row_top)
    old_scale = jnp.exp(run_max - new_max)
    new_scale = jnp.exp(row_top - new_max)
    return (
        new_max,
        run_mass * old_scale + row_total * new_scale,
        run_sum * old_scale[..., None] + partial_value * new_scale[..., None],
    )


def combine_states(first_state, second_state):
    return fold_in(first_state, second_state[0], second_state[1], second_state[2])


def row_stats(scores, kept, key_rows):
    scores = jnp.where(kept, scores, negative)
    row_top = jnp.max(scores, axis=1)
    weight = jnp.where(kept, jnp.exp(scores - row_top[:, None]), 0.0)
    partial_value = jnp.dot(
        weight.astype(jnp.bfloat16), key_rows, preferred_element_type=jnp.float32
    )
    return (row_top, jnp.sum(weight, axis=1), partial_value)


def pick_entry(table, position):
    places = jnp.arange(table.shape[0], dtype=jnp.int32)
    return jnp.sum(jnp.where(places == position, table, 0))


def empty_state(row_total, feature_count):
    return (
        jnp.full((row_total,), negative, jnp.float32),
        jnp.zeros((row_total,), jnp.float32),
        jnp.zeros((row_total, feature_count), jnp.float32),
    )


def stack_states(states):
    return tuple((jnp.stack([state[field] for state in states]) for field in range(3)))


def own_rows(stacked, slice_rows, pair_count):
    run_max, run_mass, run_sum = stacked
    local_blocks = run_max.shape[0]
    feature_count = run_sum.shape[2]
    arrived = (
        lax.all_to_all(
            run_max.reshape(local_blocks, pair_count, slice_rows),
            "pair",
            split_axis=1,
            concat_axis=1,
            tiled=True,
        ),
        lax.all_to_all(
            run_mass.reshape(local_blocks, pair_count, slice_rows),
            "pair",
            split_axis=1,
            concat_axis=1,
            tiled=True,
        ),
        lax.all_to_all(
            run_sum.reshape(local_blocks, pair_count, slice_rows, feature_count),
            "pair",
            split_axis=1,
            concat_axis=1,
            tiled=True,
        ),
    )
    new_max = jnp.max(arrived[0], axis=1)
    scales = jnp.exp(arrived[0] - new_max[:, None, :])
    return (
        new_max,
        jnp.sum(arrived[1] * scales, axis=1),
        jnp.sum(arrived[2] * scales[..., None], axis=1),
    )


def body(embeddings, cluster_sizes, row_counts):
    normed = unit_rows(embeddings)
    local_blocks, block_rows, feature_count = normed.shape
    pair_count = lax.axis_size("pair")
    own_count = lax.axis_size("own")
    block_total = own_count * local_blocks
    slice_rows = block_rows // pair_count
    own_index = lax.axis_index("own")
    slice_start = lax.axis_index("pair") * slice_rows
    my_slice = lax.dynamic_slice_in_dim(normed, slice_start, slice_rows, 1)
    cluster_start = jnp.cumsum(cluster_sizes) - cluster_sizes
    block_ids = jnp.arange(block_total, dtype=jnp.int32)
    owner_cluster = (
        jnp.sum((block_ids[:, None] >= cluster_start[None, :]).astype(jnp.int32), axis=1) - 1
    )
    full_rows = jnp.arange(block_rows, dtype=jnp.int32)
    my_rows = slice_start + jnp.arange(slice_rows, dtype=jnp.int32)
    offset_count = (SPAN + local_blocks - 2) // local_blocks

    def block_of(owner, local):
        return owner * local_blocks + local

    def linked_to(query_block, source):
        inside = (source >= 0) & (source < block_total)
        return inside & (
            pick_entry(owner_cluster, source) == pick_entry(owner_cluster, query_block)
        )

    def key_mask(query_block, source):
        valid_keys = my_rows[None, :] < pick_entry(row_counts, source)
        not_self = (query_block != source) | (full_rows[:, None] != my_rows[None, :])
        return linked_to(query_block, source) & valid_keys & not_self

    def tile_scores(queries, key_rows):
        return sharpness * jnp.dot(queries, key_rows.T, preferred_element_type=jnp.float32)

    running = [empty_state(block_rows, feature_count) for local in range(local_blocks)]
    for local in range(local_blocks):
        query_block = block_of(own_index, local)
        for other in range(local_blocks):
            source = block_of(own_index, other)
            row_top, row_total, partial_value = row_stats(
                tile_scores(normed[local], my_slice[other]),
                key_mask(query_block, source),
                my_slice[other],
            )
            running[local] = fold_in(running[local], row_top, row_total, partial_value)
    column_state = [empty_state(slice_rows, feature_count) for local in range(local_blocks)]
    for offset in range(1, offset_count + 1):
        earlier = passed_along(my_slice, "own", offset)
        back_states = [empty_state(slice_rows, feature_count) for local in range(local_blocks)]
        for local in range(local_blocks):
            query_block = block_of(own_index, local)
            query_valid = full_rows < pick_entry(row_counts, query_block)
            for other in range(local_blocks):
                source = block_of(own_index - offset, other)
                scores = tile_scores(normed[local], earlier[other])
                row_top, row_total, partial_value = row_stats(
                    scores, key_mask(query_block, source), earlier[other]
                )
                running[local] = fold_in(running[local], row_top, row_total, partial_value)
                back_mask = (
                    linked_to(query_block, source) & query_valid[None, :] & (my_rows[:, None] >= 0)
                )
                back_top, back_total, back_sum = row_stats(scores.T, back_mask, normed[local])
                back_states[other] = fold_in(back_states[other], back_top, back_total, back_sum)
        stacked_back = stack_states(back_states)
        returned = passed_along((stacked_back[0], stacked_back[1], stacked_back[2]), "own", -offset)
        later_inside = own_index + offset < own_count
        for local in range(local_blocks):
            column_state[local] = fold_in(
                column_state[local],
                jnp.where(later_inside, returned[0][local], negative),
                jnp.where(later_inside, returned[1][local], 0.0),
                jnp.where(later_inside, returned[2][local], 0.0),
            )
    reduced = own_rows(stack_states(running), slice_rows, pair_count)
    result_state = combine_states(reduced, stack_states(column_state))
    run_max, run_mass, run_sum = result_state
    my_counts = jnp.stack(
        [pick_entry(row_counts, block_of(own_index, local)) for local in range(local_blocks)]
    )
    row_valid = my_rows[None, :] < my_counts[:, None]
    near_sums = jnp.where(row_valid[..., None], run_sum / run_mass[..., None], 0.0).astype(
        jnp.bfloat16
    )
    log_masses = jnp.where(row_valid, run_max + jnp.log(run_mass), 0.0)
    return (near_sums, log_masses)


MESH = pl.DeviceIdType.MESH


def kernel(
    groups, blocks, rows, slice_rows, block_total,
    sizes_hbm, counts_hbm, emb_hbm, near_ref, mass_ref,
    sizes_ref, counts_ref, emb_ref, queries, keys, top, mass, total,
    chip_out, chip_in, chip_stats_out, chip_stats_in,
    pair_out, pair_in, pair_stats_out, pair_stats_in,
    load, share_send, share_recv, direct_send, key_recv, relay_send,
    chip_send, chip_recv, pair_send, pair_recv,
):
    width = emb_ref.shape[2]
    mine = lax.axis_index("own")
    half = lax.axis_index("pair")
    group, core = mine // 2, mine % 2
    toward = 1 - 2 * (group % 2)
    across = group + toward
    ahead, behind = group + 2 * toward, group - 2 * toward
    has_ahead = (ahead >= 0) & (ahead < groups)
    has_behind = (behind >= 0) & (behind < groups)
    behind2 = group - 4 * toward
    has_behind2 = (behind2 >= 0) & (behind2 < groups)
    slots = 2 * blocks
    half_rows = rows // 2
    core_rows = blocks * rows
    slot_keys = slots * slice_rows

    def device(group_index, core_index):
        return (group_index * 2 + core_index, half)

    partner = (mine, 1 - half)
    sibling = device(group, 1 - core)

    def half_span(side):
        return pl.ds(pl.multiple_of(side * half_rows, half_rows), half_rows)

    def load_rows(index, side):
        return pltpu.make_async_copy(
            emb_hbm.at[:, half_span(side)], emb_ref.at[:, half_span(side)], load.at[index]
        )

    load_rows(0, half).start()
    load_rows(1, 1 - half).start()
    load_sizes = pltpu.make_async_copy(sizes_hbm, sizes_ref, load.at[2])
    load_counts = pltpu.make_async_copy(counts_hbm, counts_ref, load.at[3])
    load_sizes.start()
    load_counts.start()

    barrier = pltpu.get_barrier_semaphore()

    def greet(target):
        pl.semaphore_signal(barrier, inc=1, device_id=target, device_id_type=MESH)

    greet(sibling)
    greet(partner)
    for other_core in range(2):
        greet(device(across, other_core))

    @pl.when(has_ahead)
    def _():
        for other_core in range(2):
            greet(device(ahead, other_core))

    @pl.when(has_behind)
    def _():
        for other_core in range(2):
            greet(device(behind, other_core))

    def normalise(side):
        for local in range(blocks):
            values = emb_ref[local, half_span(side), :]
            squares = jnp.sum(values * values, axis=-1, keepdims=True)
            queries[core * blocks + local, half_span(side), :] = (
                values * lax.rsqrt(squares + 1e-06)
            ).astype(jnp.bfloat16)

    load_rows(0, half).wait()
    normalise(half)

    own_blocks = pl.ds(core * blocks, blocks)
    other_blocks = pl.ds((1 - core) * blocks, blocks)

    def key_rows(core_index):
        return pl.ds(pl.multiple_of((half * 2 + core_index) * slice_rows, slice_rows), slice_rows)

    def share(index, side):
        return pltpu.make_async_remote_copy(
            src_ref=queries.at[own_blocks, half_span(side)],
            dst_ref=queries.at[own_blocks, half_span(side)],
            send_sem=share_send.at[index],
            recv_sem=share_recv.at[index],
            device_id=sibling,
            device_id_type=MESH,
        )

    def share_in(index, side):
        return pltpu.make_async_remote_copy(
            src_ref=queries.at[other_blocks, half_span(side)],
            dst_ref=queries.at[other_blocks, half_span(side)],
            send_sem=share_send.at[index],
            recv_sem=share_recv.at[index],
            device_id=sibling,
            device_id_type=MESH,
        )

    def direct(place, target, slot, other_core, local):
        block = core * blocks + local
        return pltpu.make_async_remote_copy(
            src_ref=queries.at[block, key_rows(other_core)],
            dst_ref=keys.at[slot, block],
            send_sem=direct_send.at[place, other_core, local],
            recv_sem=key_recv.at[slot, block],
            device_id=device(target, other_core),
            device_id_type=MESH,
        )

    def relay(place, source, target, slot, block):
        return pltpu.make_async_remote_copy(
            src_ref=keys.at[source, block],
            dst_ref=keys.at[slot, block],
            send_sem=relay_send.at[place, block],
            recv_sem=key_recv.at[slot, block],
            device_id=device(target, core),
            device_id_type=MESH,
        )

    def arrived(slot, block):
        relay(0, slot, across, slot, block).wait_recv()

    def direct_across(other_core, local):
        return direct(0, across, 1, other_core, local)

    def direct_ahead(other_core, local):
        return direct(1, ahead, 3, other_core, local)

    def direct_behind(other_core, local):
        return direct(2, behind, 2, other_core, local)

    skip = (1 - toward) // 2
    reach = slots - 1

    def upper(index):
        return index + 1 - skip

    def lower(index):
        return index + skip

    def relay_across(index):
        return relay(0, 2, across, 4, (index + skip) % slots)

    def relay_behind(index):
        return relay(1, 1, behind, 5, lower(index))

    def relay_ahead(index):
        return relay(2, 4, ahead, 6, upper(index))

    neighbours = 4 + 2 * has_ahead.astype(jnp.int32) + 2 * has_behind.astype(jnp.int32)
    pl.semaphore_wait(barrier, neighbours)

    for other_core in range(2):
        for local in range(blocks):
            direct_across(other_core, local).start()

            @pl.when(has_behind)
            def _():
                direct_behind(other_core, local).start()

            @pl.when(has_ahead)
            def _():
                direct_ahead(other_core, local).start()

    share(0, half).start()
    load_rows(1, 1 - half).wait()
    normalise(1 - half)
    share(1, 1 - half).start()
    load_sizes.wait()
    load_counts.wait()

    starts = []
    so_far = jnp.int32(0)
    for cluster in range(sizes_ref.shape[0]):
        starts.append(so_far)
        so_far = so_far + sizes_ref[cluster]

    def cluster_of(ids):
        return sum((ids >= start).astype(jnp.int32) for start in starts)

    top[...] = jnp.full_like(top, negative)
    mass[...] = jnp.zeros_like(mass)
    total[...] = jnp.zeros_like(total)

    @pl.when(jnp.logical_not(has_ahead))
    def _():
        keys[2] = jnp.zeros_like(keys[2])
        keys[5] = jnp.zeros_like(keys[5])

    @pl.when(jnp.logical_not(has_behind))
    def _():
        keys[3] = jnp.zeros_like(keys[3])
        keys[4] = jnp.zeros_like(keys[4])

    @pl.when(has_ahead)
    def _():
        keys[5, lower(reach) % slots] = jnp.zeros_like(keys[5, 0])

    @pl.when(has_behind2)
    def _():
        keys[6, upper(reach) % slots] = jnp.zeros_like(keys[6, 0])

    @pl.when(jnp.logical_not(has_behind2))
    def _():
        keys[6] = jnp.zeros_like(keys[6])

    own_slot = 0

    def fold(first_slot, distances, side_core):
        taken = len(distances)
        lane_ids = lax.broadcasted_iota(jnp.int32, (1, taken * slot_keys), 1)
        lane_local = lane_ids % slot_keys
        lane_row = lane_local % slice_rows + (half * 2 + core) * slice_rows
        lane_block = jnp.zeros_like(lane_ids)
        valid = jnp.zeros_like(lane_ids)
        for index, distance in enumerate(distances):
            first_block = (group + toward * distance) * slots
            for local in range(slots):
                block = first_block + local
                there = lane_ids // slice_rows == index * slots + local
                inside = (block >= 0) & (block < block_total)
                count = counts_ref[jnp.clip(block, 0, block_total - 1)]
                valid = jnp.where(there, jnp.where(inside, count, 0), valid)
                lane_block = jnp.where(there, block, lane_block)
        key_cluster = jnp.where(lane_row < valid, cluster_of(lane_block), -1)
        row_ids = lax.broadcasted_iota(jnp.int32, (core_rows, 1), 0) + (
            (group * 2 + side_core) * core_rows
        )
        query_cluster = cluster_of(row_ids // rows)
        block_keys = keys[first_slot:first_slot + taken] if isinstance(first_slot, int) else (
            keys[pl.ds(first_slot, taken)]
        )
        block_keys = block_keys.reshape(taken * slot_keys, width)
        side_blocks = pl.ds(side_core * blocks, blocks)
        span = pl.ds(pl.multiple_of(side_core * core_rows, core_rows), core_rows)
        scores = sharpness * lax.dot_general(
            queries[side_blocks].reshape(core_rows, width), block_keys,
            (((1,), (1,)), ((), ())), preferred_element_type=jnp.float32,
        )
        kept = query_cluster == key_cluster
        if first_slot is own_slot:
            kept = kept & (row_ids != lane_block * rows + lane_row)
        scores = jnp.where(kept, scores, 2.0 * negative)
        old_top = top[span]
        new_top = jnp.maximum(old_top, jnp.max(scores, axis=1, keepdims=True))
        scale = jnp.exp(old_top - new_top)
        weight = jnp.exp(scores - new_top)
        top[span] = new_top
        mass[span] = mass[span] * scale + jnp.sum(weight, axis=1, keepdims=True)
        weight = weight.astype(jnp.bfloat16)
        piece = min(256, width)
        for column in range(0, width, piece):
            columns = slice(column, column + piece)
            total[span, columns] = total[span, columns] * scale + jnp.dot(
                weight, block_keys[:, columns], preferred_element_type=jnp.float32
            )

    @pl.when(has_ahead)
    def _():
        for index in range(slots):
            arrived(2, (index + skip) % slots)
            relay_across(index).start()

    for index in range(reach):
        arrived(1, lower(index))

        @pl.when(has_behind)
        def _():
            relay_behind(index).start()

    arrived(1, lower(reach) % slots)

    share_in(0, half).wait_recv()
    keys[0] = queries[:, key_rows(core), :]
    share_in(1, 1 - half).wait_recv()

    def own_fold(side_core, carry):
        fold(own_slot, (0,), side_core)
        return carry

    lax.fori_loop(0, 2, own_fold, 0)

    def pair_fold(turn, carry):
        @pl.when((turn == 2) & has_behind)
        def _():
            for index in range(reach):
                arrived(4, upper(index))

                @pl.when(has_ahead)
                def _():
                    relay_ahead(index).start()

            arrived(4, upper(reach) % slots)
            for block in range(slots):
                arrived(3, block)

        late = turn // 2
        fold(1 + 2 * late, (1 - 3 * late, 2 - 3 * late), turn % 2)
        return carry

    lax.fori_loop(0, 4, pair_fold, 0)

    eye = (
        lax.broadcasted_iota(jnp.int32, (half_rows, half_rows), 0)
        == lax.broadcasted_iota(jnp.int32, (half_rows, half_rows), 1)
    )

    def to_lanes(column):
        return jnp.sum(jnp.where(eye, column, 0.0), axis=0, keepdims=True)

    def to_rows(lanes):
        return jnp.sum(jnp.where(eye, lanes, 0.0), axis=1, keepdims=True)

    def rows_of(block, side):
        return pl.ds(pl.multiple_of(block * rows + side * half_rows, half_rows), half_rows)

    def sent(source, target, send, recv, index, destination):
        return pltpu.make_async_remote_copy(
            src_ref=source, dst_ref=target, send_sem=send.at[index], recv_sem=recv.at[index],
            device_id=destination, device_id_type=MESH,
        )

    def chip_copy(remote):
        return sent(chip_out.at[remote], chip_in.at[remote], chip_send, chip_recv, remote, sibling)

    def pair_copy(local):
        return sent(pair_out.at[local], pair_in.at[local], pair_send, pair_recv, local, partner)

    chip_stats = sent(chip_stats_out, chip_stats_in, chip_send, chip_recv, 2, sibling)
    pair_stats = sent(pair_stats_out, pair_stats_in, pair_send, pair_recv, blocks, partner)
    sides = (1 - half, half)

    @pl.when(has_ahead)
    def _():
        for index in range(reach):
            arrived(5, lower(index))

    def late_fold(side_core, carry):
        fold(5, (3,), side_core)
        return carry

    lax.fori_loop(0, 2, late_fold, 0)

    @pl.when(has_behind2)
    def _():
        for index in range(reach):
            arrived(6, upper(index))

    def last_fold(turn, carry):
        fold(6, (-3,), jnp.where(turn == 0, 1 - core, core))

        @pl.when(turn == 0)
        def _():
            for remote in range(2):
                for local in range(blocks):
                    span = rows_of((1 - core) * blocks + local, sides[remote])
                    place = remote * blocks + local
                    chip_stats_out[place, 0:1, :half_rows] = to_lanes(top[span])
                    chip_stats_out[place, 1:2, :half_rows] = to_lanes(mass[span])
            chip_stats.start()
            for remote in range(2):
                for local in range(blocks):
                    span = rows_of((1 - core) * blocks + local, sides[remote])
                    chip_out[remote, local] = total[span].astype(jnp.bfloat16)
                chip_copy(remote).start()

        return carry

    lax.fori_loop(0, 2, last_fold, 0)

    chip_stats.wait_recv()
    scales = {}
    for remote in range(2):
        for local in range(blocks):
            span = rows_of(core * blocks + local, sides[remote])
            place = remote * blocks + local
            other_top = to_rows(chip_stats_in[place, 0:1, :half_rows])
            other_mass = to_rows(chip_stats_in[place, 1:2, :half_rows])
            new_top = jnp.maximum(top[span], other_top)
            scale = jnp.exp(top[span] - new_top)
            other_scale = jnp.exp(other_top - new_top)
            new_mass = mass[span] * scale + other_mass * other_scale
            scales[remote, local] = (scale, other_scale, new_top, new_mass)
            if remote == 0:
                pair_stats_out[local, 0:1, :half_rows] = to_lanes(new_top)
                pair_stats_out[local, 1:2, :half_rows] = to_lanes(new_mass)
    pair_stats.start()
    for remote in range(2):
        chip_copy(remote).wait_recv()
        for local in range(blocks):
            span = rows_of(core * blocks + local, sides[remote])
            scale, other_scale, new_top, new_mass = scales[remote, local]
            new_total = total[span] * scale + chip_in[remote, local].astype(jnp.float32) * other_scale
            if remote == 0:
                pair_out[local] = new_total.astype(jnp.bfloat16)
                pair_copy(local).start()
            else:
                total[span] = new_total

    place = lax.broadcasted_iota(jnp.int32, (half_rows, 1), 0) + half * half_rows
    pair_stats.wait_recv()
    final = []
    for local in range(blocks):
        other_top = to_rows(pair_stats_in[local, 0:1, :half_rows])
        other_mass = to_rows(pair_stats_in[local, 1:2, :half_rows])
        _, _, own_top, own_mass = scales[1, local]
        new_top = jnp.maximum(own_top, other_top)
        scale = jnp.exp(own_top - new_top)
        other_scale = jnp.exp(other_top - new_top)
        new_mass = own_mass * scale + other_mass * other_scale
        row_valid = place < counts_ref[mine * blocks + local]
        final.append((scale / new_mass, other_scale / new_mass, row_valid))
        logs = jnp.where(row_valid, new_top + jnp.log(new_mass), 0.0)
        mass_ref[local:local + 1, :] = to_lanes(logs)

    share(0, half).wait_send()
    share(1, 1 - half).wait_send()
    for other_core in range(2):
        for local in range(blocks):
            direct_across(other_core, local).wait_send()

            @pl.when(has_ahead)
            def _():
                direct_ahead(other_core, local).wait_send()

            @pl.when(has_behind)
            def _():
                direct_behind(other_core, local).wait_send()

    @pl.when(has_ahead)
    def _():
        for index in range(slots):
            relay_across(index).wait_send()

    @pl.when(has_behind)
    def _():
        for index in range(reach):
            relay_behind(index).wait_send()

    @pl.when(has_ahead & has_behind)
    def _():
        for index in range(reach):
            relay_ahead(index).wait_send()

    chip_stats.wait_send()
    pair_stats.wait_send()
    for remote in range(2):
        chip_copy(remote).wait_send()

    for local in range(blocks):
        pair_copy(local).wait_recv()
        span = rows_of(core * blocks + local, half)
        scale, other_scale, row_valid = final[local]
        merged = total[span] * scale + pair_in[local].astype(jnp.float32) * other_scale
        near_ref[local] = jnp.where(row_valid, merged, 0.0).astype(jnp.bfloat16)

    for local in range(blocks):
        pair_copy(local).wait_send()


def kernel_body(embeddings, cluster_sizes, row_counts):
    blocks, rows, width = embeddings.shape
    groups = lax.axis_size("own") // 2
    slots, slice_rows, half_rows = 2 * blocks, rows // 4, rows // 2
    query_rows = slots * rows
    wide, narrow = jnp.float32, jnp.bfloat16
    stats = (8, 128)
    dma = pltpu.SemaphoreType.DMA
    hbm, vmem = pl.BlockSpec(memory_space=pltpu.HBM), pl.BlockSpec(memory_space=pltpu.VMEM)
    return pl.pallas_call(
        functools.partial(kernel, groups, blocks, rows, slice_rows, row_counts.shape[0]),
        out_shape=(
            jax.ShapeDtypeStruct((blocks, half_rows, width), narrow),
            jax.ShapeDtypeStruct((blocks, half_rows), wide),
        ),
        in_specs=[hbm, hbm, hbm],
        out_specs=(vmem, vmem),
        scratch_shapes=[
            pltpu.SMEM(cluster_sizes.shape, jnp.int32),
            pltpu.SMEM(row_counts.shape, jnp.int32),
            pltpu.VMEM(embeddings.shape, wide),
            pltpu.VMEM((slots, rows, width), narrow),
            pltpu.VMEM((7, slots, slice_rows, width), narrow),
            pltpu.VMEM((query_rows, 1), wide),
            pltpu.VMEM((query_rows, 1), wide),
            pltpu.VMEM((query_rows, width), wide),
            pltpu.VMEM((2, blocks, half_rows, width), narrow),
            pltpu.VMEM((2, blocks, half_rows, width), narrow),
            pltpu.VMEM((2 * blocks, *stats), wide),
            pltpu.VMEM((2 * blocks, *stats), wide),
            pltpu.VMEM((blocks, half_rows, width), narrow),
            pltpu.VMEM((blocks, half_rows, width), narrow),
            pltpu.VMEM((blocks, *stats), wide),
            pltpu.VMEM((blocks, *stats), wide),
            dma((4,)), dma((2,)), dma((2,)),
            dma((3, 2, blocks)), dma((7, slots)), dma((3, slots)),
            dma((3,)), dma((3,)), dma((blocks + 1,)), dma((blocks + 1,)),
        ],
        compiler_params=pltpu.CompilerParams(
            collective_id=0, has_side_effects=True, vmem_limit_bytes=56 * 1024 * 1024
        ),
        cost_estimate=pl.CostEstimate(
            flops=4 * query_rows * 7 * slots * slice_rows * width,
            bytes_accessed=embeddings.size * 4,
            transcendentals=query_rows * 7 * slots * slice_rows,
        ),
    )(cluster_sizes, row_counts, embeddings)


def fits_kernel(block_shape):
    blocks, rows, width = block_shape
    covered = (SPAN + 2 * blocks - 2) // (2 * blocks) <= 3
    far_enough = 3 * 2 * blocks >= SPAN
    whole_tiles = rows % 128 == 0 and width % 128 == 0
    return lax.axis_size("pair") == 2 and lax.axis_size("own") % 4 == 0 and (
        covered and far_enough and whole_tiles
    )


def device_part(embeddings, cluster_sizes, row_counts):
    chosen = kernel_body if fits_kernel(embeddings.shape) else body
    return chosen(embeddings, cluster_sizes, row_counts)


def solution(mesh):
    placed = (P("own", None, None), P(), P())
    return jax.shard_map(
        device_part,
        mesh=mesh,
        in_specs=placed,
        out_specs=(P("own", "pair", None), P("own", "pair")),
        check_vma=False,
    )
```
